32 devices in a mesh: parts: 2 (over y), cell: 4 (over z), grp: 4 (over x, core).
Axes of the slice: x: 2, y: 2, z: 4, core: 2. Of those that a mesh axis runs over, the one named last changes fastest.
Arguments:
- sketch: bfloat16 [98304, 256], P(('parts', 'cell', 'grp')), parts along dimension 0, may hold values from -0.27063294 to 0.27063294, as said below
- slab: bfloat16 [98304, 128], P(('parts', 'cell', 'grp')), parts along dimension 0, may hold values from -6 to 6
Outputs:
- r_factor: float32 [512, 256], P('parts'), parts along dimension 0
- basis: bfloat16 [98304, 256], P(('parts', 'cell', 'grp')), parts along dimension 0
- projected: float32 [512, 128], P(('parts', 'cell'), 'grp'), parts along dimension 0
The draws below stay inside these ranges and needn't reach their ends.
There are 2 independent parts, one for each index of `parts`. The reference program is written for one: setup_inputs(seed, part) draws one part's arguments, and reference() takes and returns one part's arrays. A program takes and returns all parts, laid end to end along the dimension named above; each array names one. Nothing has to cross between parts.
Inputs may be any that keep to these rules, and one draw needn't show every extreme that they name: A scaled random sketch of full column rank.
All inputs are finite; a program needn't handle non-finite values.
Results may differ from the reference program's by a relative error of at most 0.001.
Values sent between devices are 32-bit elements; how exact they have to be, the bound alone decides.
No kernel may reach another device: no remote copies, remote signals or barrier semaphores. Data moves between devices by JAX's collectives and lax.ppermute only.
A program may use at most 64 MiB of HBM per device.

```python
import jax
import jax.numpy as jnp
from jax import lax

ROW_DEV = 3072
K = 256
SLAB = 128
ROWS = 49152


def draw_sketch(key, part):
    key_base, key_rows, key_cols = jax.random.split(jax.random.fold_in(key, 17), 3)
    positions = jnp.arange(ROWS, dtype=jnp.float32)
    trend = 1.0 + 2.0 * positions / ROWS
    row_scale = jnp.exp(jax.random.uniform(key_rows, (ROWS,), jnp.float32, 0.0, jnp.log(10.0)))
    col_scale = jnp.exp(jax.random.uniform(key_cols, (K,), jnp.float32, jnp.log(0.5), jnp.log(2.0)))
    base = jnp.clip(jax.random.normal(key_base, (ROWS, K), jnp.float32), -4.0, 4.0)
    values = base * (row_scale * trend)[:, None] * col_scale[None, :] / (4.0 * jnp.sqrt(ROWS * 1.0))
    return values.astype(jnp.bfloat16)


def levels(stream_key, shape, cuts, low, largest):
    level = 1.0
    for position, blocks in cuts:
        steps = jax.random.uniform(jax.random.fold_in(jax.random.fold_in(stream_key, 6), position), (blocks,), jnp.float32, low / len(cuts), largest / len(cuts))
        level = level * jnp.repeat(jnp.exp(steps), shape[position] // blocks).reshape((-1,) + (1,) * (len(shape) - 1 - position))
    return level


def gaussian(key, dims, deviation, limit, shards=(), kind=jnp.bfloat16):
    values = jax.random.normal(key, dims, jnp.float32) * deviation
    if len(shards) > 0:
        values = levels(key, dims, shards, -0.22, 0.18) * values
    return jnp.clip(values, min=-limit, max=limit).astype(kind)


def setup_inputs(seed: int = 0, part: int = 0) -> dict:
    arg_keys = jax.random.split(jax.random.key(seed), 3)
    part_keys = jax.random.split(jax.random.fold_in(arg_keys[2], part), 3)
    sketch = draw_sketch(jax.random.fold_in(jax.random.fold_in(arg_keys[2], part), 71), part)
    slab = gaussian(part_keys[1], (ROWS, SLAB), 1.0, 6.0, ((0, 16),))
    return {"sketch": sketch, "slab": slab}


def gram_of(piece):
    return lax.dot_general(piece.astype(jnp.float32), piece.astype(jnp.float32), (((0,), (0,)), ((), ())), preferred_element_type=jnp.float32)

def reference(sketch, slab):
    sketch_blocks = sketch.reshape(ROWS // ROW_DEV, ROW_DEV, K)
    slab_blocks = slab.reshape(ROWS // ROW_DEV, ROW_DEV, SLAB)

    def add_stats(totals, pieces):
        rows_block, slab_block = pieces
        gram_part = gram_of(rows_block)
        cross_part = lax.dot_general(rows_block.astype(jnp.float32), slab_block.astype(jnp.float32), (((0,), (0,)), ((), ())), preferred_element_type=jnp.float32)
        return ((totals[0] + gram_part, totals[1] + cross_part), None)
    start_totals = (jnp.zeros((K, K), jnp.float32), jnp.zeros((K, SLAB), jnp.float32))
    totals, unused = lax.scan(add_stats, start_totals, (sketch_blocks, slab_blocks))
    gram_sum, cross_sum = totals
    lower_factor = jnp.linalg.cholesky(gram_sum)
    identity = jnp.eye(K, dtype=jnp.float32)
    inverse_lower = lax.linalg.triangular_solve(lower_factor, identity, left_side=True, lower=True)
    inverse_upper = inverse_lower.T

    def solve_block(rows_block):
        exact_rows = jnp.dot(rows_block.astype(jnp.float32), inverse_upper.astype(jnp.float32), precision=lax.Precision.HIGHEST, preferred_element_type=jnp.float32)
        return exact_rows.astype(jnp.bfloat16)
    basis = lax.map(solve_block, sketch_blocks).reshape(ROWS, K)
    projected = lax.linalg.triangular_solve(lower_factor, cross_sum, left_side=True, lower=True)
    return (lower_factor.T, basis, projected)
```

```python
import functools

import jax
import jax.numpy as jnp
from jax import lax
from jax.experimental import pallas as pl
from jax.experimental.pallas import tpu as pltpu
from jax.sharding import PartitionSpec as P

SUB, LANES = 8, 128
HIGHEST = lax.Precision.HIGHEST


def chunks_of(rows, wanted):
    while rows % (16 * wanted):
        wanted -= 1
    return wanted


def stats_kernel(steps, sketch_hbm, slab_hbm, gram_ref, cross_ref, sketch, slab, sems):
    size = sketch.shape[0] // steps
    copies = []
    for step in range(steps):
        rows = pl.ds(step * size, size)
        pair = []
        for which, (src, dst) in enumerate(((sketch_hbm, sketch), (slab_hbm, slab))):
            copy = pltpu.make_async_copy(src.at[rows], dst.at[rows], sems.at[which, step])
            copy.start()
            pair.append(copy)
        copies.append(pair)
    contract = (((0,), (0,)), ((), ()))
    for step in range(steps):
        rows = pl.ds(step * size, size)
        for copy in copies[step]:
            copy.wait()
        part = sketch[rows, :]
        gram = lax.dot_general(part, part, contract, preferred_element_type=jnp.float32)
        cross = lax.dot_general(slab[rows, :], part, contract, preferred_element_type=jnp.float32)
        if step:
            gram, cross = gram_ref[...] + gram, cross_ref[...] + cross
        gram_ref[...] = gram
        cross_ref[...] = cross


def local_stats(sketch, slab):
    rows, k = sketch.shape
    days = slab.shape[1]
    steps = chunks_of(rows, 6)
    hbm = pl.BlockSpec(memory_space=pl.ANY)
    vmem = pl.BlockSpec(memory_space=pltpu.VMEM)
    return pl.pallas_call(
        functools.partial(stats_kernel, steps),
        out_shape=(
            jax.ShapeDtypeStruct((k, k), jnp.float32),
            jax.ShapeDtypeStruct((days, k), jnp.float32),
        ),
        in_specs=[hbm, hbm],
        out_specs=(vmem, vmem),
        scratch_shapes=[
            pltpu.VMEM((rows, k), sketch.dtype),
            pltpu.VMEM((rows, days), slab.dtype),
            pltpu.SemaphoreType.DMA((2, steps)),
        ],
        name="local_stats",
    )(sketch, slab)


def eliminate(a_ref, r_ref, x_ref):
    k = a_ref.shape[0]
    halves = k // LANES
    shape = (SUB, LANES)
    sub = lax.broadcasted_iota(jnp.int32, shape, 0)
    lane = lax.broadcasted_iota(jnp.int32, shape, 1)

    def load(panel):
        rows = pl.ds(panel * SUB, SUB)
        return [a_ref[rows, pl.ds(h * LANES, LANES)] for h in range(halves)]

    def row_of(v, i):
        return jnp.broadcast_to(v[i : i + 1, :], shape)

    def column_of(v, i):
        return jnp.broadcast_to(v[:, i : i + 1], shape)

    for panel in range(k // SUB):
        half, first = divmod(panel * SUB, LANES)
        block = load(panel)
        cols = [column_of(block[half], first + i) for i in range(SUB)]
        saved = [jnp.zeros(shape, jnp.float32)] * halves
        scale = jnp.zeros(shape, jnp.float32)
        for i in range(SUB):
            here = sub == i
            pivot = row_of(cols[i], i)
            inverse = 1.0 / pivot
            root = lax.rsqrt(pivot)
            scale = jnp.where(here, root, scale)
            saved = [jnp.where(here, b, s) for b, s in zip(block, saved)]
            unit = jnp.where(here, 1.0, 0.0)
            block[half] = jnp.where(lane == first + i, unit, block[half])

            def step(v):
                row = row_of(v, i)
                return jnp.where(here, row * inverse, v - (cols[i] * row) * inverse)

            for j in range(i + 1, SUB):
                cols[j] = step(cols[j])
            block = [step(b) for b in block]
        rows = pl.ds(panel * SUB, SUB)
        for h in range(halves):
            at = pl.ds(h * LANES, LANES)
            ahead = lane + h * LANES - (sub + panel * SUB)
            z = saved[h] * scale
            r_ref[rows, at] = jnp.where(ahead >= 0, z, 0.0)
            x_ref[rows, at] = jnp.where(ahead < 0, z, jnp.where(ahead == 0, scale, 0.0))
        pivots = [[row_of(b, i) for b in block] for i in range(SUB)]
        inside = (lane >= first) & (lane < first + SUB)
        for other in range(panel + 1, k // SUB):
            target = load(other)
            coefs = [column_of(target[half], first + i) for i in range(SUB)]
            target[half] = jnp.where(inside, 0.0, target[half])
            rows = pl.ds(other * SUB, SUB)
            for h in range(halves):
                total = coefs[0] * pivots[0][h]
                for i in range(1, SUB):
                    total = total + coefs[i] * pivots[i][h]
                a_ref[rows, pl.ds(h * LANES, LANES)] = target[h] - total


def split3(v):
    high = v.astype(jnp.bfloat16)
    rest = v - high.astype(jnp.float32)
    middle = rest.astype(jnp.bfloat16)
    low = (rest - middle.astype(jnp.float32)).astype(jnp.bfloat16)
    return high, middle, low


def factor_kernel(
    steps, cells, mine_ref, theirs_ref, cross_ref, sketch_hbm, r_ref, basis_hbm, proj_ref,
    a_ref, x_ref, sketch, basis, sem_in, sems,
):
    copy_in = pltpu.make_async_copy(sketch_hbm, sketch, sem_in)
    copy_in.start()
    k = a_ref.shape[0]
    n = k // 2
    core = lax.axis_index("grp") % 2
    first = core == 0
    square = jnp.where(first, mine_ref[0:n, :], theirs_ref[0:n, :])
    packed = jnp.where(first, theirs_ref[0:n, :], mine_ref[0:n, :])
    diagonal = jnp.where(first, theirs_ref[n : n + 1, :], mine_ref[n : n + 1, :])
    turned = packed.T
    row = lax.broadcasted_iota(jnp.int32, (n, n), 0)
    col = lax.broadcasted_iota(jnp.int32, (n, n), 1)
    a_ref[0:n, 0:n] = jnp.where(row >= col, packed, turned)
    a_ref[0:n, n:k] = square.T
    a_ref[n:k, 0:n] = square
    a_ref[n:k, n:k] = jnp.where(
        row < col, packed, jnp.where(row > col, turned, jnp.broadcast_to(diagonal, (n, n)))
    )
    eliminate(a_ref, r_ref, x_ref)
    x = x_ref[...]
    count = k // cells
    start = pl.multiple_of(lax.axis_index("cell") * count, count)
    proj_ref[...] = lax.dot_general(
        x_ref[pl.ds(start, count), :],
        cross_ref[...],
        (((1,), (1,)), ((), ())),
        precision=HIGHEST,
        preferred_element_type=jnp.float32,
    )
    parts = split3(x)
    copy_in.wait()
    size = sketch.shape[0] // steps
    copies = []
    for step in range(steps):
        rows = pl.ds(step * size, size)
        piece = sketch[rows, :]
        total = None
        for part in parts[::-1]:
            term = lax.dot_general(
                piece, part, (((1,), (1,)), ((), ())), preferred_element_type=jnp.float32
            )
            total = term if total is None else total + term
        basis[rows, :] = total.astype(basis.dtype)
        copy = pltpu.make_async_copy(basis.at[rows], basis_hbm.at[rows], sems.at[step])
        copy.start()
        copies.append(copy)
    for copy in copies:
        copy.wait()


def factor(mine, theirs, cross, sketch, cells):
    rows, k = sketch.shape
    steps = chunks_of(rows, 6)
    hbm = pl.BlockSpec(memory_space=pl.ANY)
    vmem = pl.BlockSpec(memory_space=pltpu.VMEM)
    return pl.pallas_call(
        functools.partial(factor_kernel, steps, cells),
        out_shape=(
            jax.ShapeDtypeStruct((k, k), jnp.float32),
            jax.ShapeDtypeStruct((rows, k), jnp.bfloat16),
            jax.ShapeDtypeStruct((k // cells, cross.shape[0]), jnp.float32),
        ),
        in_specs=[vmem, vmem, vmem, hbm],
        out_specs=(vmem, hbm, vmem),
        scratch_shapes=[
            pltpu.VMEM((k, k), jnp.float32),
            pltpu.VMEM((k, k), jnp.float32),
            pltpu.VMEM((rows, k), sketch.dtype),
            pltpu.VMEM((rows, k), jnp.bfloat16),
            pltpu.SemaphoreType.DMA,
            pltpu.SemaphoreType.DMA((steps,)),
        ],
        name="factor",
    )(mine, theirs, cross, sketch)


def swap(value, axis, bit):
    size = lax.axis_size(axis)
    return lax.ppermute(value, axis, [(i, i ^ bit) for i in range(size)])


def halve(days, place, bit):
    groups, rows, k = days.shape
    pairs = days.reshape(groups // 2, 2, rows, k)
    own = (place // bit) % 2
    return (
        lax.dynamic_index_in_dim(pairs, own, 1, keepdims=False),
        lax.dynamic_index_in_dim(pairs, 1 - own, 1, keepdims=False),
    )


def flat(gram, days):
    groups, rows, k = days.shape
    days = days.reshape(groups * rows, k)
    return jnp.concatenate([gram] + [days[:, i : i + LANES] for i in range(0, k, LANES)], 0)


def unflat(both, gram_rows, groups, rows, k):
    count = groups * rows
    days = [both[gram_rows + i * count : gram_rows + (i + 1) * count] for i in range(k // LANES)]
    return both[:gram_rows], jnp.concatenate(days, 1).reshape(groups, rows, k)


def local(sketch, slab):
    cells, groups = lax.axis_size("cell"), lax.axis_size("grp")
    place = lax.axis_index("grp")
    gram, days = local_stats(sketch, slab)
    k = gram.shape[0]
    n = k // 2
    top, low, square = gram[:n, :n], gram[n:, n:], gram[n:, :n]
    row = lax.broadcasted_iota(jnp.int32, (n, n), 0)
    col = lax.broadcasted_iota(jnp.int32, (n, n), 1)
    packed = jnp.where(row >= col, top, low)
    diagonal = jnp.sum(jnp.where(row == col, low, 0.0), axis=0, keepdims=True)
    extra = jnp.broadcast_to(diagonal, (SUB, n))
    halves = jnp.stack([jnp.concatenate([square, extra], 0), jnp.concatenate([packed, extra], 0)])
    core = place % 2
    kept = lax.dynamic_index_in_dim(halves, core, 0, keepdims=False)
    sent = lax.dynamic_index_in_dim(halves, 1 - core, 0, keepdims=False)
    days = days.reshape(groups, days.shape[0] // groups, k)
    bit = 1
    while bit < groups:
        days_kept, days_sent = halve(days, place, bit)
        if bit == 1:
            gram_kept, gram_sent = kept, sent
        else:
            gram_kept = gram_sent = kept
        got = swap(flat(gram_sent, days_sent), "grp", bit)
        both = flat(gram_kept, days_kept) + got
        kept, days = unflat(both, gram_kept.shape[0], *days_kept.shape)
        bit *= 2
    bit = 1
    while bit < cells:
        both = both + swap(both, "cell", bit)
        bit *= 2
    kept, days = unflat(both, kept.shape[0], *days.shape)
    theirs = swap(kept, "grp", 1)
    r_factor, basis, projected = factor(kept, theirs, days[0], sketch, cells)
    return r_factor, basis, projected


def solution(mesh):
    in_specs = (P(("parts", "cell", "grp"), None), P(("parts", "cell", "grp"), None))
    out_specs = (P("parts", None), P(("parts", "cell", "grp"), None), P(("parts", "cell"), "grp"))
    return jax.shard_map(local, mesh=mesh, in_specs=in_specs, out_specs=out_specs, check_vma=False)
```

```python
import functools

import jax
import jax.numpy as jnp
from jax import lax
from jax.experimental import pallas as pl
from jax.experimental.pallas import tpu as pltpu
from jax.sharding import PartitionSpec as P

SUB, LANES = 8, 128
VMEM_LIMIT = 24 * 2**20
HIGHEST = lax.Precision.HIGHEST


def chunks_of(rows, wanted):
    while rows % (16 * wanted):
        wanted -= 1
    return wanted


def stats_kernel(
    steps, groups, sketch_hbm, slab_hbm, kept_ref, sent_ref, sketch, slab, gram_ref, cross_ref, sems
):
    size = sketch.shape[0] // steps
    copies = []
    for step in range(steps):
        rows = pl.ds(step * size, size)
        pair = []
        for which, (src, dst) in enumerate(((sketch_hbm, sketch), (slab_hbm, slab))):
            copy = pltpu.make_async_copy(src.at[rows], dst.at[rows], sems.at[which, step])
            copy.start()
            pair.append(copy)
        copies.append(pair)
    contract = (((0,), (0,)), ((), ()))
    for step in range(steps):
        rows = pl.ds(step * size, size)
        for copy in copies[step]:
            copy.wait()
        part = sketch[rows, :]
        gram = lax.dot_general(part, part, contract, preferred_element_type=jnp.float32)
        cross = lax.dot_general(slab[rows, :], part, contract, preferred_element_type=jnp.float32)
        if step:
            gram, cross = gram_ref[...] + gram, cross_ref[...] + cross
        gram_ref[...] = gram
        cross_ref[...] = cross
    k = gram_ref.shape[0]
    n = k // 2
    first = lax.axis_index("grp") % 2 == 0
    row = lax.broadcasted_iota(jnp.int32, (n, n), 0)
    col = lax.broadcasted_iota(jnp.int32, (n, n), 1)
    square, top, low = gram_ref[n:k, 0:n], gram_ref[0:n, 0:n], gram_ref[n:k, n:k]
    packed = jnp.where(row >= col, top, low)
    diagonal = jnp.sum(jnp.where(row == col, low, 0.0), axis=0, keepdims=True)
    kept_ref[0:n, :] = jnp.where(first, square, packed)
    sent_ref[0:n, :] = jnp.where(first, packed, square)
    for ref in (kept_ref, sent_ref):
        ref[n : n + SUB, :] = jnp.broadcast_to(diagonal, (SUB, n))
    count = cross_ref.shape[0] // groups
    at = n + SUB
    for pair in range(groups // 2):
        even = pl.ds(2 * pair * count, count)
        odd = pl.ds((2 * pair + 1) * count, count)
        for lanes in (pl.ds(h, LANES) for h in range(0, k, LANES)):
            rows = pl.ds(at, count)
            kept_ref[rows, :] = jnp.where(first, cross_ref[even, lanes], cross_ref[odd, lanes])
            sent_ref[rows, :] = jnp.where(first, cross_ref[odd, lanes], cross_ref[even, lanes])
            at += count


def local_stats(sketch, slab, groups):
    rows, k = sketch.shape
    days = slab.shape[1]
    steps = chunks_of(rows, 6)
    hbm = pl.BlockSpec(memory_space=pltpu.HBM)
    vmem = pl.BlockSpec(memory_space=pltpu.VMEM)
    out = jax.ShapeDtypeStruct((k // 2 + SUB + days // 2 * (k // LANES), LANES), jnp.float32)
    return pl.pallas_call(
        functools.partial(stats_kernel, steps, groups),
        out_shape=(out, out),
        in_specs=[hbm, hbm],
        out_specs=(vmem, vmem),
        scratch_shapes=[
            pltpu.VMEM((rows, k), sketch.dtype),
            pltpu.VMEM((rows, days), slab.dtype),
            pltpu.VMEM((k, k), jnp.float32),
            pltpu.VMEM((days, k), jnp.float32),
            pltpu.SemaphoreType.DMA((2, steps)),
        ],
        compiler_params=pltpu.CompilerParams(vmem_limit_bytes=VMEM_LIMIT),
        name="local_stats",
    )(sketch, slab)


def eliminate(a_ref, r_ref, x_ref):
    k = a_ref.shape[0]
    halves = k // LANES
    shape = (SUB, LANES)
    sub = lax.broadcasted_iota(jnp.int32, shape, 0)
    lane = lax.broadcasted_iota(jnp.int32, shape, 1)

    def load(panel):
        rows = pl.ds(panel * SUB, SUB)
        return [a_ref[rows, pl.ds(h * LANES, LANES)] for h in range(halves)]

    def row_of(v, i):
        return jnp.broadcast_to(v[i : i + 1, :], shape)

    def column_of(v, i):
        return jnp.broadcast_to(v[:, i : i + 1], shape)

    for panel in range(k // SUB):
        half, first = divmod(panel * SUB, LANES)
        block = load(panel)
        cols = [column_of(block[half], first + i) for i in range(SUB)]
        saved = [jnp.zeros(shape, jnp.float32)] * halves
        scale = jnp.zeros(shape, jnp.float32)
        for i in range(SUB):
            here = sub == i
            pivot = row_of(cols[i], i)
            inverse = 1.0 / pivot
            root = lax.rsqrt(pivot)
            scale = jnp.where(here, root, scale)
            saved = [jnp.where(here, b, s) for b, s in zip(block, saved)]
            unit = jnp.where(here, 1.0, 0.0)
            block[half] = jnp.where(lane == first + i, unit, block[half])

            def step(v):
                row = row_of(v, i)
                return jnp.where(here, row * inverse, v - (cols[i] * row) * inverse)

            for j in range(i + 1, SUB):
                cols[j] = step(cols[j])
            block = [step(b) for b in block]
        rows = pl.ds(panel * SUB, SUB)
        for h in range(halves):
            at = pl.ds(h * LANES, LANES)
            ahead = lane + h * LANES - (sub + panel * SUB)
            z = saved[h] * scale
            r_ref[rows, at] = jnp.where(ahead >= 0, z, 0.0)
            x_ref[rows, at] = jnp.where(ahead < 0, z, jnp.where(ahead == 0, scale, 0.0))
        pivots = [[row_of(b, i) for b in block] for i in range(SUB)]
        inside = (lane >= first) & (lane < first + SUB)
        for other in range(panel + 1, k // SUB):
            target = load(other)
            coefs = [column_of(target[half], first + i) for i in range(SUB)]
            target[half] = jnp.where(inside, 0.0, target[half])
            rows = pl.ds(other * SUB, SUB)
            for h in range(halves):
                total = coefs[0] * pivots[0][h]
                for i in range(1, SUB):
                    total = total + coefs[i] * pivots[i][h]
                a_ref[rows, pl.ds(h * LANES, LANES)] = target[h] - total


def split3(v):
    high = v.astype(jnp.bfloat16)
    rest = v - high.astype(jnp.float32)
    middle = rest.astype(jnp.bfloat16)
    low = (rest - middle.astype(jnp.float32)).astype(jnp.bfloat16)
    return high, middle, low


def factor_kernel(
    steps, cells, mine_ref, theirs_ref, sketch_hbm, r_ref, basis_hbm, proj_ref,
    a_ref, x_ref, sketch, basis, sem_in, sems,
):
    copy_in = pltpu.make_async_copy(sketch_hbm, sketch, sem_in)
    copy_in.start()
    k = a_ref.shape[0]
    n = k // 2
    core = lax.axis_index("grp") % 2
    first = core == 0
    square = jnp.where(first, mine_ref[0:n, :], theirs_ref[0:n, :])
    packed = jnp.where(first, theirs_ref[0:n, :], mine_ref[0:n, :])
    diagonal = jnp.where(first, theirs_ref[n : n + 1, :], mine_ref[n : n + 1, :])
    turned = packed.T
    row = lax.broadcasted_iota(jnp.int32, (n, n), 0)
    col = lax.broadcasted_iota(jnp.int32, (n, n), 1)
    a_ref[0:n, 0:n] = jnp.where(row >= col, packed, turned)
    a_ref[0:n, n:k] = square.T
    a_ref[n:k, 0:n] = square
    a_ref[n:k, n:k] = jnp.where(
        row < col, packed, jnp.where(row > col, turned, jnp.broadcast_to(diagonal, (n, n)))
    )
    eliminate(a_ref, r_ref, x_ref)
    count = k // cells
    start = pl.multiple_of(lax.axis_index("cell") * count, count)
    own_rows = pl.ds(start, count)
    days = proj_ref.shape[0]
    total = None
    for h in range(k // LANES):
        at = n + SUB + h * days
        term = lax.dot_general(
            mine_ref[at : at + days, :],
            x_ref[own_rows, h * LANES : (h + 1) * LANES],
            (((1,), (1,)), ((), ())),
            precision=HIGHEST,
            preferred_element_type=jnp.float32,
        )
        total = term if total is None else total + term
    proj_ref[...] = total
    parts = split3(x_ref[...])
    copy_in.wait()
    size = sketch.shape[0] // steps
    copies = []
    for step in range(steps):
        rows = pl.ds(step * size, size)
        piece = sketch[rows, :]
        total = None
        for part in parts[::-1]:
            term = lax.dot_general(
                piece, part, (((1,), (1,)), ((), ())), preferred_element_type=jnp.float32
            )
            total = term if total is None else total + term
        basis[rows, :] = total.astype(basis.dtype)
        copy = pltpu.make_async_copy(basis.at[rows], basis_hbm.at[rows], sems.at[step])
        copy.start()
        copies.append(copy)
    for copy in copies:
        copy.wait()


def factor(mine, theirs, sketch, cells):
    rows, k = sketch.shape
    days = (mine.shape[0] - theirs.shape[0]) * LANES // k
    steps = chunks_of(rows, 6)
    hbm = pl.BlockSpec(memory_space=pltpu.HBM)
    vmem = pl.BlockSpec(memory_space=pltpu.VMEM)
    return pl.pallas_call(
        functools.partial(factor_kernel, steps, cells),
        out_shape=(
            jax.ShapeDtypeStruct((k, k), jnp.float32),
            jax.ShapeDtypeStruct((rows, k), jnp.bfloat16),
            jax.ShapeDtypeStruct((days, k // cells), jnp.float32),
        ),
        in_specs=[vmem, vmem, hbm],
        out_specs=(vmem, hbm, vmem),
        scratch_shapes=[
            pltpu.VMEM((k, k), jnp.float32),
            pltpu.VMEM((k, k), jnp.float32),
            pltpu.VMEM((rows, k), sketch.dtype),
            pltpu.VMEM((rows, k), jnp.bfloat16),
            pltpu.SemaphoreType.DMA,
            pltpu.SemaphoreType.DMA((steps,)),
        ],
        compiler_params=pltpu.CompilerParams(vmem_limit_bytes=VMEM_LIMIT),
        name="factor",
    )(mine, theirs, sketch)


def swap(value, axis, bit):
    size = lax.axis_size(axis)
    return lax.ppermute(value, axis, [(i, i ^ bit) for i in range(size)])


def local(sketch, slab):
    cells, groups = lax.axis_size("cell"), lax.axis_size("grp")
    place = lax.axis_index("grp")
    shared = sketch.shape[1] // 2 + SUB
    kept, sent = local_stats(sketch, slab, groups)
    both = kept + swap(sent, "grp", 1)
    bit = 2
    while bit < groups:
        gram, days = both[:shared], both[shared:]
        days = days.reshape(groups // (2 * bit), 2, -1, LANES)
        own = (place // bit) % 2
        kept_days = lax.dynamic_index_in_dim(days, own, 1, keepdims=False).reshape(-1, LANES)
        sent_days = lax.dynamic_index_in_dim(days, 1 - own, 1, keepdims=False).reshape(-1, LANES)
        got = swap(jnp.concatenate([gram, sent_days], 0), "grp", bit)
        both = jnp.concatenate([gram, kept_days], 0) + got
        bit *= 2
    bit = 1
    while bit < cells:
        both = both + swap(both, "cell", bit)
        bit *= 2
    theirs = swap(both[:shared], "grp", 1)
    r_factor, basis, projected = factor(both, theirs, sketch, cells)
    return r_factor, basis, projected.T


def solution(mesh):
    in_specs = (P(("parts", "cell", "grp"), None), P(("parts", "cell", "grp"), None))
    out_specs = (P("parts", None), P(("parts", "cell", "grp"), None), P(("parts", "cell"), "grp"))
    return jax.shard_map(local, mesh=mesh, in_specs=in_specs, out_specs=out_specs, check_vma=False)
```

```python
import functools

import jax
import jax.numpy as jnp
from jax import lax
from jax.experimental import pallas as pl
from jax.experimental.pallas import tpu as pltpu
from jax.sharding import PartitionSpec as P

SUB, LANES = 8, 128
VMEM_LIMIT = 24 * 2**20
STATS_LIMIT = 56 * 10**6
HIGHEST = lax.Precision.HIGHEST


def chunks_of(rows, wanted):
    while rows % (16 * wanted):
        wanted -= 1
    return wanted


def stats_kernel(
    steps, groups, sketch_hbm, slab_hbm, kept_ref, sent_ref, sketch, slab, gram_ref, cross_ref, sems
):
    size = sketch.shape[0] // steps
    copies = []
    for step in range(steps):
        rows = pl.ds(step * size, size)
        pair = []
        for which, (src, dst) in enumerate(((sketch_hbm, sketch), (slab_hbm, slab))):
            copy = pltpu.make_async_copy(src.at[rows], dst.at[rows], sems.at[which, step])
            copy.start()
            pair.append(copy)
        copies.append(pair)
    contract = (((0,), (0,)), ((), ()))
    for step in range(steps):
        rows = pl.ds(step * size, size)
        for copy in copies[step]:
            copy.wait()
        part = sketch[rows, :]
        gram = lax.dot_general(part, part, contract, preferred_element_type=jnp.float32)
        cross = lax.dot_general(slab[rows, :], part, contract, preferred_element_type=jnp.float32)
        if step:
            gram, cross = gram_ref[...] + gram, cross_ref[...] + cross
        gram_ref[...] = gram
        cross_ref[...] = cross
    k = gram_ref.shape[0]
    n = k // 2
    first = lax.axis_index("grp") % 2 == 0
    row = lax.broadcasted_iota(jnp.int32, (n, n), 0)
    col = lax.broadcasted_iota(jnp.int32, (n, n), 1)
    square, top, low = gram_ref[n:k, 0:n], gram_ref[0:n, 0:n], gram_ref[n:k, n:k]
    packed = jnp.where(row >= col, top, low)
    diagonal = jnp.sum(jnp.where(row == col, low, 0.0), axis=0, keepdims=True)
    kept_ref[0:n, :] = jnp.where(first, square, packed)
    sent_ref[0:n, :] = jnp.where(first, packed, square)
    for ref in (kept_ref, sent_ref):
        ref[n : n + SUB, :] = jnp.broadcast_to(diagonal, (SUB, n))
    count = cross_ref.shape[0] // groups
    at = n + SUB
    for pair in range(groups // 2):
        even = pl.ds(2 * pair * count, count)
        odd = pl.ds((2 * pair + 1) * count, count)
        for lanes in (pl.ds(h, LANES) for h in range(0, k, LANES)):
            rows = pl.ds(at, count)
            kept_ref[rows, :] = jnp.where(first, cross_ref[even, lanes], cross_ref[odd, lanes])
            sent_ref[rows, :] = jnp.where(first, cross_ref[odd, lanes], cross_ref[even, lanes])
            at += count


def local_stats(sketch, slab, groups):
    rows, k = sketch.shape
    days = slab.shape[1]
    steps = chunks_of(rows, 3)
    hbm = pl.BlockSpec(memory_space=pltpu.HBM)
    vmem = pl.BlockSpec(memory_space=pltpu.VMEM)
    out = jax.ShapeDtypeStruct((k // 2 + SUB + days // 2 * (k // LANES), LANES), jnp.float32)
    return pl.pallas_call(
        functools.partial(stats_kernel, steps, groups),
        out_shape=(out, out),
        in_specs=[hbm, hbm],
        out_specs=(vmem, vmem),
        scratch_shapes=[
            pltpu.VMEM((rows, k), sketch.dtype),
            pltpu.VMEM((rows, days), slab.dtype),
            pltpu.VMEM((k, k), jnp.float32),
            pltpu.VMEM((days, k), jnp.float32),
            pltpu.SemaphoreType.DMA((2, steps)),
        ],
        compiler_params=pltpu.CompilerParams(vmem_limit_bytes=STATS_LIMIT),
        name="local_stats",
    )(sketch, slab)


def tree_sum(terms):
    while len(terms) > 1:
        odd = terms[len(terms) & ~1 :]
        terms = [x + y for x, y in zip(terms[::2], terms[1::2])] + odd
    return terms[0]


def split3(v):
    high = v.astype(jnp.bfloat16)
    rest = v - high.astype(jnp.float32)
    middle = rest.astype(jnp.bfloat16)
    low = (rest - middle.astype(jnp.float32)).astype(jnp.bfloat16)
    return high, middle, low


def eliminate(a_ref, one_ref, scale, unscale, r_ref, x_ref):
    k = a_ref.shape[0]
    halves, panels = k // LANES, k // SUB
    shape = (SUB, LANES)
    sub = lax.broadcasted_iota(jnp.int32, shape, 0)
    lane = lax.broadcasted_iota(jnp.int32, shape, 1)
    here = [sub == i for i in range(SUB)]
    one = one_ref[...]

    def rows_of(panel):
        return pl.ds(panel * SUB, SUB)

    def lanes_of(half):
        return pl.ds(half * LANES, LANES)

    def load(panel):
        return [a_ref[rows_of(panel), lanes_of(h)] for h in range(halves)]

    def row_of(v, i):
        return jnp.broadcast_to(v[i : i + 1, :], shape)

    def column_of(v, i):
        return jnp.broadcast_to(v[:, i : i + 1], shape)

    def follow(target, panel, pivots):
        half, first = divmod(panel * SUB, LANES)
        coefs = [column_of(target[half], first + i) for i in range(SUB)]
        inside = (lane >= first) & (lane < first + SUB)
        rest = list(target)
        rest[half] = jnp.where(inside, 0.0, rest[half])
        return [
            rest[h] - tree_sum([coefs[i] * pivots[i][h] for i in range(SUB)]) for h in range(halves)
        ]

    def solve(panel, block):
        half, first = divmod(panel * SUB, LANES)
        block = list(block)
        cols = [column_of(block[half], first + i) * one for i in range(SUB)]
        saved = [jnp.zeros(shape, jnp.float32)] * halves
        roots = jnp.zeros(shape, jnp.float32)
        for i in range(0, SUB, 2):
            upper, lower = here[i], here[i + 1]
            both = upper | lower
            p, q, r = row_of(cols[i], i), row_of(cols[i + 1], i), row_of(cols[i + 1], i + 1)
            det = p * r - q * q
            inverse = 1.0 / det
            over = 1.0 / p
            roots = jnp.where(
                both, jnp.where(upper, lax.rsqrt(p), lax.rsqrt(det * over)), roots
            )
            ratio = jnp.where(lower, q * over, 0.0)
            for h in range(halves):
                z = block[h] - ratio * row_of(block[h], i)
                if h == half:
                    z = jnp.where((lane == first + i) & lower, -ratio, z)
                saved[h] = jnp.where(both, z, saved[h])
            left = jnp.where(upper, -1.0, jnp.where(lower, 0.0, cols[i]))
            right = jnp.where(upper, 0.0, jnp.where(lower, -1.0, cols[i + 1]))
            on_upper = left * r - right * q
            on_lower = right * p - left * q

            def step(v):
                change = row_of(v, i) * on_upper + row_of(v, i + 1) * on_lower
                return jnp.where(both, 0.0, v) - change * inverse

            unit = jnp.where(
                lane == first + i, jnp.where(upper, 1.0, 0.0), jnp.where(lower, 1.0, 0.0)
            )
            pair = (lane == first + i) | (lane == first + i + 1)
            block[half] = jnp.where(pair, unit, block[half])
            cols = [step(c) if j > i + 1 else c for j, c in enumerate(cols)]
            block = [step(v) for v in block]
        for h in range(halves):
            ahead = lane + h * LANES - (sub + panel * SUB)
            z = saved[h] * roots
            inverse_part = jnp.where(ahead < 0, z, jnp.where(ahead == 0, roots, 0.0))
            r_ref[rows_of(panel), lanes_of(h)] = jnp.where(ahead >= 0, z, 0.0) * unscale[h]
            x_ref[rows_of(panel), lanes_of(h)] = inverse_part * scale[h]
        return block

    per = 4
    size = per * SUB
    blocks = k // size
    lanes_all = lax.broadcasted_iota(jnp.int32, (size, k), 1)
    panel_all = lax.broadcasted_iota(jnp.int32, (size, k), 0) // SUB
    ahead_block = None
    for number in range(blocks):
        befores, afters = [], []
        for panel in range(number * per, (number + 1) * per):
            before = load(panel) if ahead_block is None else ahead_block
            after = solve(panel, before)
            befores.append(jnp.concatenate(before, 1))
            afters.append(jnp.concatenate(after, 1))
            pivots = [[row_of(v, i) for v in after] for i in range(SUB)]
            for other in range(panel + 1, min((number + 2) * per, panels)):
                target = follow(load(other), panel, pivots)
                if other == panel + 1:
                    ahead_block = target
                    continue
                for h in range(halves):
                    a_ref[rows_of(other), lanes_of(h)] = target[h]
        if number + 2 >= blocks:
            continue
        low = number * size
        top = (number + 2) * size
        base = top // LANES * LANES
        lhs = split3(jnp.concatenate(befores, 0)[:, base:])
        later = (lanes_all < low + size) & (lanes_all >= low + (panel_all + 1) * SUB)
        rhs = split3(jnp.where(later, 0.0, jnp.concatenate(afters, 0)))
        change = lax.dot_general(
            jnp.concatenate([lhs[i] for i in (0, 0, 1, 0, 2, 1)], 0),
            jnp.concatenate([rhs[i] for i in (0, 1, 0, 2, 0, 1)], 0),
            (((0,), (0,)), ((), ())),
            preferred_element_type=jnp.float32,
        )[top - base :]
        lanes = lax.broadcasted_iota(jnp.int32, (k - top, k), 1)
        inside = (lanes >= low) & (lanes < low + size)
        a_ref[top:k, :] = jnp.where(inside, 0.0, a_ref[top:k, :]) - change


def factor_kernel(
    steps, cells, mine_ref, theirs_ref, sketch_hbm, r_hbm, basis_hbm, proj_hbm,
    a_ref, one_ref, r_ref, x_ref, proj_ref, sketch, basis, sem_in, sem_r, sem_proj, sems,
):
    copy_in = pltpu.make_async_copy(sketch_hbm, sketch, sem_in)
    copy_in.start()
    k = a_ref.shape[0]
    n = k // 2
    one_ref[...] = jnp.ones_like(one_ref)
    first = lax.axis_index("grp") % 2 == 0
    square = jnp.where(first, mine_ref[0:n, :], theirs_ref[0:n, :])
    packed = jnp.where(first, theirs_ref[0:n, :], mine_ref[0:n, :])
    row = lax.broadcasted_iota(jnp.int32, (n, n), 0)
    col = lax.broadcasted_iota(jnp.int32, (n, n), 1)
    norms = [
        jnp.sum(jnp.where(row == col, packed, 0.0), axis=0, keepdims=True),
        mine_ref[n : n + 1, :],
    ]
    scale = [lax.rsqrt(v) for v in norms]
    unscale = [v * s for v, s in zip(norms, scale)]
    turned = jnp.where(row >= col, packed * scale[0], packed * scale[1]).T
    turned = jnp.where(row <= col, turned * scale[0], turned * scale[1])
    packed = turned.T
    a_ref[0:n, 0:n] = jnp.where(row >= col, packed, turned)
    a_ref[n:k, n:k] = jnp.where(row < col, packed, jnp.where(row > col, turned, 1.0))
    square = (square * scale[0]).T * scale[1]
    a_ref[0:n, n:k] = square
    a_ref[n:k, 0:n] = square.T
    eliminate(a_ref, one_ref, scale, unscale, r_ref, x_ref)
    copy_r = pltpu.make_async_copy(r_ref, r_hbm, sem_r)
    copy_r.start()
    copies = [copy_r]
    parts = split3(x_ref[...])
    copy_in.wait()
    size = sketch.shape[0] // steps
    for step in range(steps):
        rows = pl.ds(step * size, size)
        piece = sketch[rows, :]
        total = None
        for part in parts[::-1]:
            term = lax.dot_general(
                piece, part, (((1,), (1,)), ((), ())), preferred_element_type=jnp.float32
            )
            total = term if total is None else total + term
        basis[rows, :] = total.astype(basis.dtype)
        copy = pltpu.make_async_copy(basis.at[rows], basis_hbm.at[rows], sems.at[step])
        copy.start()
        copies.append(copy)
        if step:
            continue
        count = k // cells
        own_rows = pl.ds(pl.multiple_of(lax.axis_index("cell") * count, count), count)
        days = proj_ref.shape[0]
        total = None
        for h in range(k // LANES):
            at = n + SUB + h * days
            term = lax.dot_general(
                mine_ref[at : at + days, :],
                x_ref[own_rows, h * LANES : (h + 1) * LANES],
                (((1,), (1,)), ((), ())),
                precision=HIGHEST,
                preferred_element_type=jnp.float32,
            )
            total = term if total is None else total + term
        proj_ref[...] = total
        copy = pltpu.make_async_copy(proj_ref, proj_hbm, sem_proj)
        copy.start()
        copies.append(copy)
    for copy in copies:
        copy.wait()


def factor(mine, theirs, sketch, cells):
    rows, k = sketch.shape
    days = (mine.shape[0] - theirs.shape[0]) * LANES // k
    steps = chunks_of(rows, 6)
    hbm = pl.BlockSpec(memory_space=pltpu.HBM)
    vmem = pl.BlockSpec(memory_space=pltpu.VMEM)
    return pl.pallas_call(
        functools.partial(factor_kernel, steps, cells),
        out_shape=(
            jax.ShapeDtypeStruct((k, k), jnp.float32),
            jax.ShapeDtypeStruct((rows, k), jnp.bfloat16),
            jax.ShapeDtypeStruct((days, k // cells), jnp.float32),
        ),
        in_specs=[vmem, vmem, hbm],
        out_specs=(hbm, hbm, hbm),
        scratch_shapes=[
            pltpu.VMEM((k, k), jnp.float32),
            pltpu.VMEM((SUB, LANES), jnp.float32),
            pltpu.VMEM((k, k), jnp.float32),
            pltpu.VMEM((k, k), jnp.float32),
            pltpu.VMEM((days, k // cells), jnp.float32),
            pltpu.VMEM((rows, k), sketch.dtype),
            pltpu.VMEM((rows, k), jnp.bfloat16),
            pltpu.SemaphoreType.DMA,
            pltpu.SemaphoreType.DMA,
            pltpu.SemaphoreType.DMA,
            pltpu.SemaphoreType.DMA((steps,)),
        ],
        compiler_params=pltpu.CompilerParams(vmem_limit_bytes=VMEM_LIMIT),
        name="factor",
    )(mine, theirs, sketch)


def swap(value, axis, bit):
    size = lax.axis_size(axis)
    return lax.ppermute(value, axis, [(i, i ^ bit) for i in range(size)])


def local(sketch, slab):
    cells, groups = lax.axis_size("cell"), lax.axis_size("grp")
    place = lax.axis_index("grp")
    shared = sketch.shape[1] // 2 + SUB
    kept, sent = local_stats(sketch, slab, groups)
    both = kept + swap(sent, "grp", 1)
    bit = 2
    while bit < groups:
        gram, days = both[:shared], both[shared:]
        days = days.reshape(groups // (2 * bit), 2, -1, LANES)
        own = (place // bit) % 2
        kept_days = lax.dynamic_index_in_dim(days, own, 1, keepdims=False).reshape(-1, LANES)
        sent_days = lax.dynamic_index_in_dim(days, 1 - own, 1, keepdims=False).reshape(-1, LANES)
        got = swap(jnp.concatenate([gram, sent_days], 0), "grp", bit)
        both = jnp.concatenate([gram, kept_days], 0) + got
        bit *= 2
    bit = 1
    while bit < cells:
        both = both + swap(both, "cell", bit)
        bit *= 2
    theirs = swap(both[:shared], "grp", 1)
    r_factor, basis, projected = factor(both, theirs, sketch, cells)
    return r_factor, basis, projected.T


def solution(mesh):
    in_specs = (P(("parts", "cell", "grp"), None), P(("parts", "cell", "grp"), None))
    out_specs = (P("parts", None), P(("parts", "cell", "grp"), None), P(("parts", "cell"), "grp"))
    return jax.shard_map(local, mesh=mesh, in_specs=in_specs, out_specs=out_specs, check_vma=False)
```

```python
import functools

import jax
import jax.numpy as jnp
from jax import lax
from jax.experimental import pallas as pl
from jax.experimental.pallas import tpu as pltpu
from jax.sharding import PartitionSpec as P

SUB, LANES = 8, 128
VMEM_LIMIT = 24 * 2**20
STATS_LIMIT = 56 * 10**6
HIGHEST = lax.Precision.HIGHEST


def chunks_of(rows, wanted):
    while rows % (16 * wanted):
        wanted -= 1
    return wanted


def stats_kernel(
    steps, groups, sketch_hbm, slab_hbm, kept_ref, sent_ref, sketch, slab, gram_ref, cross_ref, sems
):
    size = sketch.shape[0] // steps
    copies = []
    for step in range(steps):
        rows = pl.ds(step * size, size)
        pair = []
        for which, (src, dst) in enumerate(((sketch_hbm, sketch), (slab_hbm, slab))):
            copy = pltpu.make_async_copy(src.at[rows], dst.at[rows], sems.at[which, step])
            copy.start()
            pair.append(copy)
        copies.append(pair)
    contract = (((0,), (0,)), ((), ()))
    for step in range(steps):
        rows = pl.ds(step * size, size)
        for copy in copies[step]:
            copy.wait()
        part = sketch[rows, :]
        gram = lax.dot_general(part, part, contract, preferred_element_type=jnp.float32)
        cross = lax.dot_general(slab[rows, :], part, contract, preferred_element_type=jnp.float32)
        if step:
            gram, cross = gram_ref[...] + gram, cross_ref[...] + cross
        gram_ref[...] = gram
        cross_ref[...] = cross
    k = gram_ref.shape[0]
    n = k // 2
    first = lax.axis_index("grp") % 2 == 0
    row = lax.broadcasted_iota(jnp.int32, (n, n), 0)
    col = lax.broadcasted_iota(jnp.int32, (n, n), 1)
    square, top, low = gram_ref[n:k, 0:n], gram_ref[0:n, 0:n], gram_ref[n:k, n:k]
    packed = jnp.where(row >= col, top, low)
    norms = [jnp.sum(jnp.where(row == col, v, 0.0), axis=0, keepdims=True) for v in (top, low)]
    tile = lax.broadcasted_iota(jnp.int32, (SUB, n), 0)
    diagonal = jnp.where(tile == 0, norms[0], jnp.where(tile == 1, norms[1], 0.0))
    kept_ref[0:n, :] = jnp.where(first, square, packed)
    sent_ref[0:n, :] = jnp.where(first, packed, square)
    for ref in (kept_ref, sent_ref):
        ref[n : n + SUB, :] = diagonal
    count = cross_ref.shape[0] // groups
    at = n + SUB
    for pair in range(groups // 2):
        even = pl.ds(2 * pair * count, count)
        odd = pl.ds((2 * pair + 1) * count, count)
        for lanes in (pl.ds(h, LANES) for h in range(0, k, LANES)):
            rows = pl.ds(at, count)
            kept_ref[rows, :] = jnp.where(first, cross_ref[even, lanes], cross_ref[odd, lanes])
            sent_ref[rows, :] = jnp.where(first, cross_ref[odd, lanes], cross_ref[even, lanes])
            at += count


def local_stats(sketch, slab, groups):
    rows, k = sketch.shape
    days = slab.shape[1]
    steps = chunks_of(rows, 3)
    hbm = pl.BlockSpec(memory_space=pltpu.HBM)
    vmem = pl.BlockSpec(memory_space=pltpu.VMEM)
    out = jax.ShapeDtypeStruct((k // 2 + SUB + days // 2 * (k // LANES), LANES), jnp.float32)
    return pl.pallas_call(
        functools.partial(stats_kernel, steps, groups),
        out_shape=(out, out),
        in_specs=[hbm, hbm],
        out_specs=(vmem, vmem),
        scratch_shapes=[
            pltpu.VMEM((rows, k), sketch.dtype),
            pltpu.VMEM((rows, days), slab.dtype),
            pltpu.VMEM((k, k), jnp.float32),
            pltpu.VMEM((days, k), jnp.float32),
            pltpu.SemaphoreType.DMA((2, steps)),
        ],
        compiler_params=pltpu.CompilerParams(vmem_limit_bytes=STATS_LIMIT),
        name="local_stats",
    )(sketch, slab)


def tree_sum(terms):
    while len(terms) > 1:
        odd = terms[len(terms) & ~1 :]
        terms = [x + y for x, y in zip(terms[::2], terms[1::2])] + odd
    return terms[0]


def split3(v):
    high = v.astype(jnp.bfloat16)
    rest = v - high.astype(jnp.float32)
    middle = rest.astype(jnp.bfloat16)
    low = (rest - middle.astype(jnp.float32)).astype(jnp.bfloat16)
    return high, middle, low


def eliminate(a_ref, one_ref, scale, unscale, r_ref, x_ref):
    k = a_ref.shape[0]
    halves, panels = k // LANES, k // SUB
    shape = (SUB, LANES)
    sub = lax.broadcasted_iota(jnp.int32, shape, 0)
    lane = lax.broadcasted_iota(jnp.int32, shape, 1)
    here = [sub == i for i in range(SUB)]
    one = one_ref[...]

    def rows_of(panel):
        return pl.ds(panel * SUB, SUB)

    def lanes_of(half):
        return pl.ds(half * LANES, LANES)

    def load(panel):
        return [a_ref[rows_of(panel), lanes_of(h)] for h in range(halves)]

    def row_of(v, i):
        return jnp.broadcast_to(v[i : i + 1, :], shape)

    def column_of(v, i):
        return jnp.broadcast_to(v[:, i : i + 1], shape)

    def follow(target, panel, pivots):
        half, first = divmod(panel * SUB, LANES)
        coefs = [column_of(target[half], first + i) for i in range(SUB)]
        inside = (lane >= first) & (lane < first + SUB)
        rest = list(target)
        rest[half] = jnp.where(inside, 0.0, rest[half])
        return [
            rest[h] - tree_sum([coefs[i] * pivots[i][h] for i in range(SUB)]) for h in range(halves)
        ]

    def solve(panel, block):
        half, first = divmod(panel * SUB, LANES)
        block = list(block)
        cols = [column_of(block[half], first + i) * one for i in range(SUB)]
        saved = [jnp.zeros(shape, jnp.float32)] * halves
        roots = jnp.zeros(shape, jnp.float32)
        for i in range(0, SUB, 2):
            upper, lower = here[i], here[i + 1]
            both = upper | lower
            p, q, r = row_of(cols[i], i), row_of(cols[i + 1], i), row_of(cols[i + 1], i + 1)
            det = p * r - q * q
            inverse = 1.0 / det
            over = 1.0 / p
            roots = jnp.where(
                both, jnp.where(upper, lax.rsqrt(p), lax.rsqrt(det * over)), roots
            )
            ratio = jnp.where(lower, q * over, 0.0)
            for h in range(halves):
                z = block[h] - ratio * row_of(block[h], i)
                if h == half:
                    z = jnp.where((lane == first + i) & lower, -ratio, z)
                saved[h] = jnp.where(both, z, saved[h])
            left = jnp.where(upper, -1.0, jnp.where(lower, 0.0, cols[i]))
            right = jnp.where(upper, 0.0, jnp.where(lower, -1.0, cols[i + 1]))
            on_upper = left * r - right * q
            on_lower = right * p - left * q

            def step(v):
                change = row_of(v, i) * on_upper + row_of(v, i + 1) * on_lower
                return jnp.where(both, 0.0, v) - change * inverse

            unit = jnp.where(
                lane == first + i, jnp.where(upper, 1.0, 0.0), jnp.where(lower, 1.0, 0.0)
            )
            pair = (lane == first + i) | (lane == first + i + 1)
            block[half] = jnp.where(pair, unit, block[half])
            cols = [step(c) if j > i + 1 else c for j, c in enumerate(cols)]
            block = [step(v) for v in block]
        for h in range(halves):
            ahead = lane + h * LANES - (sub + panel * SUB)
            z = saved[h] * roots
            inverse_part = jnp.where(ahead < 0, z, jnp.where(ahead == 0, roots, 0.0))
            r_ref[rows_of(panel), lanes_of(h)] = jnp.where(ahead >= 0, z, 0.0) * unscale[h]
            x_ref[rows_of(panel), lanes_of(h)] = inverse_part * scale[h]
        return block

    per = 4
    size = per * SUB
    blocks = k // size
    lanes_all = lax.broadcasted_iota(jnp.int32, (size, k), 1)
    panel_all = lax.broadcasted_iota(jnp.int32, (size, k), 0) // SUB
    ahead_block = None
    for number in range(blocks):
        befores, afters = [], []
        for panel in range(number * per, (number + 1) * per):
            before = load(panel) if ahead_block is None else ahead_block
            after = solve(panel, before)
            befores.append(jnp.concatenate(before, 1))
            afters.append(jnp.concatenate(after, 1))
            pivots = [[row_of(v, i) for v in after] for i in range(SUB)]
            for other in range(panel + 1, min((number + 2) * per, panels)):
                target = follow(load(other), panel, pivots)
                if other == panel + 1:
                    ahead_block = target
                    continue
                for h in range(halves):
                    a_ref[rows_of(other), lanes_of(h)] = target[h]
        if number + 2 >= blocks:
            continue
        low = number * size
        top = (number + 2) * size
        base = top // LANES * LANES
        lhs = split3(jnp.concatenate(befores, 0)[:, base:])
        later = (lanes_all < low + size) & (lanes_all >= low + (panel_all + 1) * SUB)
        rhs = split3(jnp.where(later, 0.0, jnp.concatenate(afters, 0)))
        change = lax.dot_general(
            jnp.concatenate([lhs[i] for i in (0, 0, 1, 0, 2, 1)], 0),
            jnp.concatenate([rhs[i] for i in (0, 1, 0, 2, 0, 1)], 0),
            (((0,), (0,)), ((), ())),
            preferred_element_type=jnp.float32,
        )[top - base :]
        lanes = lax.broadcasted_iota(jnp.int32, (k - top, k), 1)
        inside = (lanes >= low) & (lanes < low + size)
        a_ref[top:k, :] = jnp.where(inside, 0.0, a_ref[top:k, :]) - change


def factor_kernel(
    steps, cells, mine_ref, theirs_ref, sketch_hbm, r_hbm, basis_hbm, proj_hbm,
    a_ref, one_ref, r_ref, x_ref, proj_ref, sketch, basis, sem_in, sem_r, sem_proj, sems,
):
    copy_in = pltpu.make_async_copy(sketch_hbm, sketch, sem_in)
    copy_in.start()
    k = a_ref.shape[0]
    n = k // 2
    one_ref[...] = jnp.ones_like(one_ref)
    first = lax.axis_index("grp") % 2 == 0
    square = jnp.where(first, mine_ref[0:n, :], theirs_ref[0:n, :])
    packed = jnp.where(first, theirs_ref[0:n, :], mine_ref[0:n, :])
    row = lax.broadcasted_iota(jnp.int32, (n, n), 0)
    col = lax.broadcasted_iota(jnp.int32, (n, n), 1)
    norms = [mine_ref[n + i : n + i + 1, :] for i in range(2)]
    scale = [lax.rsqrt(v) for v in norms]
    unscale = [v * s for v, s in zip(norms, scale)]
    across = [jnp.broadcast_to(s, (n, n)) for s in scale]
    down = [s.T for s in across]
    turned = packed.T
    a_ref[0:n, 0:n] = jnp.where(row >= col, packed, turned) * across[0] * down[0]
    below = jnp.where(row < col, packed, turned) * across[1] * down[1]
    a_ref[n:k, n:k] = jnp.where(row == col, 1.0, below)
    a_ref[0:n, n:k] = square.T * across[1] * down[0]
    a_ref[n:k, 0:n] = square * across[0] * down[1]
    eliminate(a_ref, one_ref, scale, unscale, r_ref, x_ref)
    copy_r = pltpu.make_async_copy(r_ref, r_hbm, sem_r)
    copy_r.start()
    copies = [copy_r]
    parts = split3(x_ref[...])
    copy_in.wait()
    size = sketch.shape[0] // steps
    for step in range(steps):
        rows = pl.ds(step * size, size)
        piece = sketch[rows, :]
        total = None
        for part in parts[::-1]:
            term = lax.dot_general(
                piece, part, (((1,), (1,)), ((), ())), preferred_element_type=jnp.float32
            )
            total = term if total is None else total + term
        basis[rows, :] = total.astype(basis.dtype)
        copy = pltpu.make_async_copy(basis.at[rows], basis_hbm.at[rows], sems.at[step])
        copy.start()
        copies.append(copy)
        if step:
            continue
        count = k // cells
        own_rows = pl.ds(pl.multiple_of(lax.axis_index("cell") * count, count), count)
        days = proj_ref.shape[0]
        total = None
        for h in range(k // LANES):
            at = n + SUB + h * days
            term = lax.dot_general(
                mine_ref[at : at + days, :],
                x_ref[own_rows, h * LANES : (h + 1) * LANES],
                (((1,), (1,)), ((), ())),
                precision=HIGHEST,
                preferred_element_type=jnp.float32,
            )
            total = term if total is None else total + term
        proj_ref[...] = total
        copy = pltpu.make_async_copy(proj_ref, proj_hbm, sem_proj)
        copy.start()
        copies.append(copy)
    for copy in copies:
        copy.wait()


def factor(mine, theirs, sketch, cells):
    rows, k = sketch.shape
    days = (mine.shape[0] - theirs.shape[0]) * LANES // k
    steps = chunks_of(rows, 6)
    hbm = pl.BlockSpec(memory_space=pltpu.HBM)
    vmem = pl.BlockSpec(memory_space=pltpu.VMEM)
    return pl.pallas_call(
        functools.partial(factor_kernel, steps, cells),
        out_shape=(
            jax.ShapeDtypeStruct((k, k), jnp.float32),
            jax.ShapeDtypeStruct((rows, k), jnp.bfloat16),
            jax.ShapeDtypeStruct((days, k // cells), jnp.float32),
        ),
        in_specs=[vmem, vmem, hbm],
        out_specs=(hbm, hbm, hbm),
        scratch_shapes=[
            pltpu.VMEM((k, k), jnp.float32),
            pltpu.VMEM((SUB, LANES), jnp.float32),
            pltpu.VMEM((k, k), jnp.float32),
            pltpu.VMEM((k, k), jnp.float32),
            pltpu.VMEM((days, k // cells), jnp.float32),
            pltpu.VMEM((rows, k), sketch.dtype),
            pltpu.VMEM((rows, k), jnp.bfloat16),
            pltpu.SemaphoreType.DMA,
            pltpu.SemaphoreType.DMA,
            pltpu.SemaphoreType.DMA,
            pltpu.SemaphoreType.DMA((steps,)),
        ],
        compiler_params=pltpu.CompilerParams(vmem_limit_bytes=VMEM_LIMIT),
        name="factor",
    )(mine, theirs, sketch)


def swap(value, axis, bit):
    size = lax.axis_size(axis)
    return lax.ppermute(value, axis, [(i, i ^ bit) for i in range(size)])


def local(sketch, slab):
    cells, groups = lax.axis_size("cell"), lax.axis_size("grp")
    place = lax.axis_index("grp")
    shared = sketch.shape[1] // 2 + SUB
    kept, sent = local_stats(sketch, slab, groups)
    both = kept + swap(sent, "grp", 1)
    bit = 2
    while bit < groups:
        gram, days = both[:shared], both[shared:]
        days = days.reshape(groups // (2 * bit), 2, -1, LANES)
        own = (place // bit) % 2
        kept_days = lax.dynamic_index_in_dim(days, own, 1, keepdims=False).reshape(-1, LANES)
        sent_days = lax.dynamic_index_in_dim(days, 1 - own, 1, keepdims=False).reshape(-1, LANES)
        got = swap(jnp.concatenate([gram, sent_days], 0), "grp", bit)
        both = jnp.concatenate([gram, kept_days], 0) + got
        bit *= 2
    bit = 1
    while bit < cells:
        both = both + swap(both, "cell", bit)
        bit *= 2
    theirs = swap(both[:shared], "grp", 1)
    r_factor, basis, projected = factor(both, theirs, sketch, cells)
    return r_factor, basis, projected.T


def solution(mesh):
    in_specs = (P(("parts", "cell", "grp"), None), P(("parts", "cell", "grp"), None))
    out_specs = (P("parts", None), P(("parts", "cell", "grp"), None), P(("parts", "cell"), "grp"))
    return jax.shard_map(local, mesh=mesh, in_specs=in_specs, out_specs=out_specs, check_vma=False)
```

```python
import functools

import jax
import jax.numpy as jnp
from jax import lax
from jax.experimental import pallas as pl
from jax.experimental.pallas import tpu as pltpu
from jax.sharding import PartitionSpec as P

SUB, LANES = 8, 128
VMEM_LIMIT = 24 * 2**20
STATS_LIMIT = 56 * 10**6
HIGHEST = lax.Precision.HIGHEST


def chunks_of(rows, wanted):
    while rows % (16 * wanted):
        wanted -= 1
    return wanted


def stats_kernel(
    steps, groups, sketch_hbm, slab_hbm, kept_ref, sent_ref, sketch, slab, gram_ref, cross_ref, sems
):
    size = sketch.shape[0] // steps
    copies = []
    for step in range(steps):
        rows = pl.ds(step * size, size)
        pair = []
        for which, (src, dst) in enumerate(((sketch_hbm, sketch), (slab_hbm, slab))):
            copy = pltpu.make_async_copy(src.at[rows], dst.at[rows], sems.at[which, step])
            copy.start()
            pair.append(copy)
        copies.append(pair)
    contract = (((0,), (0,)), ((), ()))
    for step in range(steps):
        rows = pl.ds(step * size, size)
        for copy in copies[step]:
            copy.wait()
        part = sketch[rows, :]
        gram = lax.dot_general(part, part, contract, preferred_element_type=jnp.float32)
        cross = lax.dot_general(slab[rows, :], part, contract, preferred_element_type=jnp.float32)
        if step:
            gram, cross = gram_ref[...] + gram, cross_ref[...] + cross
        gram_ref[...] = gram
        cross_ref[...] = cross
    k = gram_ref.shape[0]
    n = k // 2
    first = lax.axis_index("grp") % 2 == 0
    row = lax.broadcasted_iota(jnp.int32, (n, n), 0)
    col = lax.broadcasted_iota(jnp.int32, (n, n), 1)
    square, top, low = gram_ref[n:k, 0:n], gram_ref[0:n, 0:n], gram_ref[n:k, n:k]
    packed = jnp.where(row >= col, top, low)
    norms = [jnp.sum(jnp.where(row == col, v, 0.0), axis=0, keepdims=True) for v in (top, low)]
    tile = lax.broadcasted_iota(jnp.int32, (SUB, n), 0)
    diagonal = jnp.where(tile == 0, norms[0], jnp.where(tile == 1, norms[1], 0.0))
    kept_ref[0:n, :] = jnp.where(first, square, packed)
    sent_ref[0:n, :] = jnp.where(first, packed, square)
    for ref in (kept_ref, sent_ref):
        ref[n : n + SUB, :] = diagonal
    count = cross_ref.shape[0] // groups
    at = n + SUB
    for pair in range(groups // 2):
        even = pl.ds(2 * pair * count, count)
        odd = pl.ds((2 * pair + 1) * count, count)
        for lanes in (pl.ds(h, LANES) for h in range(0, k, LANES)):
            rows = pl.ds(at, count)
            kept_ref[rows, :] = jnp.where(first, cross_ref[even, lanes], cross_ref[odd, lanes])
            sent_ref[rows, :] = jnp.where(first, cross_ref[odd, lanes], cross_ref[even, lanes])
            at += count


def local_stats(sketch, slab, groups):
    rows, k = sketch.shape
    days = slab.shape[1]
    steps = chunks_of(rows, 3)
    hbm = pl.BlockSpec(memory_space=pltpu.HBM)
    vmem = pl.BlockSpec(memory_space=pltpu.VMEM)
    out = jax.ShapeDtypeStruct((k // 2 + SUB + days // 2 * (k // LANES), LANES), jnp.float32)
    return pl.pallas_call(
        functools.partial(stats_kernel, steps, groups),
        out_shape=(out, out),
        in_specs=[hbm, hbm],
        out_specs=(vmem, vmem),
        scratch_shapes=[
            pltpu.VMEM((rows, k), sketch.dtype),
            pltpu.VMEM((rows, days), slab.dtype),
            pltpu.VMEM((k, k), jnp.float32),
            pltpu.VMEM((days, k), jnp.float32),
            pltpu.SemaphoreType.DMA((2, steps)),
        ],
        compiler_params=pltpu.CompilerParams(vmem_limit_bytes=STATS_LIMIT),
        name="local_stats",
    )(sketch, slab)


def tree_sum(terms):
    while len(terms) > 1:
        odd = terms[len(terms) & ~1 :]
        terms = [x + y for x, y in zip(terms[::2], terms[1::2])] + odd
    return terms[0]


def split3(v):
    high = v.astype(jnp.bfloat16)
    rest = v - high.astype(jnp.float32)
    middle = rest.astype(jnp.bfloat16)
    low = (rest - middle.astype(jnp.float32)).astype(jnp.bfloat16)
    return high, middle, low


def eliminate(a_ref, one_ref, r_ref, x_ref, meanwhile=None):
    k = a_ref.shape[0]
    halves, panels = k // LANES, k // SUB
    shape = (SUB, LANES)
    sub = lax.broadcasted_iota(jnp.int32, shape, 0)
    lane = lax.broadcasted_iota(jnp.int32, shape, 1)
    here = [sub == i for i in range(SUB)]
    one = one_ref[...]

    def rows_of(panel):
        return pl.ds(panel * SUB, SUB)

    def lanes_of(half):
        return pl.ds(half * LANES, LANES)

    def load(panel):
        return [a_ref[rows_of(panel), lanes_of(h)] for h in range(halves)]

    def row_of(v, i):
        return jnp.broadcast_to(v[i : i + 1, :], shape)

    def column_of(v, i):
        return jnp.broadcast_to(v[:, i : i + 1], shape)

    def follow(target, panel, pivots, coefs=None):
        half, first = divmod(panel * SUB, LANES)
        if coefs is None:
            coefs = [column_of(target[half], first + i) for i in range(SUB)]
        inside = (lane >= first) & (lane < first + SUB)
        rest = list(target)
        rest[half] = jnp.where(inside, 0.0, rest[half])
        return [
            rest[h] - tree_sum([coefs[i] * pivots[i][h] for i in range(SUB)]) for h in range(halves)
        ]

    def columns(panel, block):
        half, first = divmod(panel * SUB, LANES)
        return [column_of(block[half], first + i) * one for i in range(SUB)]

    def solve(panel, block, cols, under=None, corner=None):
        half, first = divmod(panel * SUB, LANES)
        block, cols = list(block), list(cols)
        saved = [jnp.zeros(shape, jnp.float32)] * halves
        roots = jnp.zeros(shape, jnp.float32)
        for i in range(0, SUB, 2):
            upper, lower = here[i], here[i + 1]
            both = upper | lower
            p, q, r = row_of(cols[i], i), row_of(cols[i + 1], i), row_of(cols[i + 1], i + 1)
            det = p * r - q * q
            inverse = 1.0 / det
            over = 1.0 / p
            roots = jnp.where(
                both, jnp.where(upper, lax.rsqrt(p), lax.rsqrt(det * over)), roots
            )
            ratio = jnp.where(lower, q * over, 0.0)
            for h in range(halves):
                z = block[h] - ratio * row_of(block[h], i)
                if h == half:
                    z = jnp.where((lane == first + i) & lower, -ratio, z)
                saved[h] = jnp.where(both, z, saved[h])
            left = jnp.where(upper, -1.0, jnp.where(lower, 0.0, cols[i]))
            right = jnp.where(upper, 0.0, jnp.where(lower, -1.0, cols[i + 1]))
            on_upper = left * r - right * q
            on_lower = right * p - left * q

            def step(v):
                change = row_of(v, i) * on_upper + row_of(v, i + 1) * on_lower
                return jnp.where(both, 0.0, v) - change * inverse

            unit = jnp.where(
                lane == first + i, jnp.where(upper, 1.0, 0.0), jnp.where(lower, 1.0, 0.0)
            )
            pair = (lane == first + i) | (lane == first + i + 1)
            block[half] = jnp.where(pair, unit, block[half])
            if under is not None:
                left, right = under[i], under[i + 1]
                by_upper = left * r - right * q
                by_lower = right * p - left * q

                def step_under(v, upper_value, lower_value):
                    return v - (upper_value * by_upper + lower_value * by_lower) * inverse

                corner = [
                    step_under(c, row_of(left, j), row_of(right, j)) for j, c in enumerate(corner)
                ]
                under = [
                    step_under(u, row_of(cols[j], i), row_of(cols[j], i + 1)) if j > i + 1 else u
                    for j, u in enumerate(under)
                ]
            cols = [step(c) if j > i + 1 else c for j, c in enumerate(cols)]
            block = [step(v) for v in block]
        for h in range(halves):
            ahead = lane + h * LANES - (sub + panel * SUB)
            z = saved[h] * roots
            inverse_part = jnp.where(ahead < 0, z, jnp.where(ahead == 0, roots, 0.0))
            r_ref[rows_of(panel), lanes_of(h)] = jnp.where(ahead >= 0, z, 0.0)
            x_ref[rows_of(panel), lanes_of(h)] = inverse_part
        return block, corner

    per = 4
    size = per * SUB
    blocks = k // size
    lanes_all = lax.broadcasted_iota(jnp.int32, (size, k), 1)
    panel_all = lax.broadcasted_iota(jnp.int32, (size, k), 0) // SUB
    ahead_block = None
    for number in range(blocks):
        befores, afters = [], []
        for panel in range(number * per, (number + 1) * per):
            before = load(panel) if ahead_block is None else ahead_block
            if panel % 2 == 0:
                lower = load(panel + 1)
                under = columns(panel, lower)
                after, corner = solve(
                    panel, before, columns(panel, before), under, columns(panel + 1, lower)
                )
            else:
                under = None
                after, _ = solve(panel, before, corner)
            befores.append(jnp.concatenate(before, 1))
            afters.append(jnp.concatenate(after, 1))
            pivots = [[row_of(v, i) for v in after] for i in range(SUB)]
            for other in range(panel + 1, min((number + 2) * per, panels)):
                target = follow(load(other), panel, pivots, under if other == panel + 1 else None)
                if other == panel + 1:
                    ahead_block = target
                    continue
                for h in range(halves):
                    a_ref[rows_of(other), lanes_of(h)] = target[h]
            if meanwhile is not None:
                meanwhile(panel)
        if number + 2 >= blocks:
            continue
        low = number * size
        top = (number + 2) * size
        base = top // LANES * LANES
        lhs = split3(jnp.concatenate(befores, 0)[:, base:])
        later = (lanes_all < low + size) & (lanes_all >= low + (panel_all + 1) * SUB)
        rhs = split3(jnp.where(later, 0.0, jnp.concatenate(afters, 0)))
        change = lax.dot_general(
            jnp.concatenate([lhs[i] for i in (0, 0, 1, 0, 2, 1)], 0),
            jnp.concatenate([rhs[i] for i in (0, 1, 0, 2, 0, 1)], 0),
            (((0,), (0,)), ((), ())),
            preferred_element_type=jnp.float32,
        )[top - base :]
        lanes = lax.broadcasted_iota(jnp.int32, (k - top, k), 1)
        inside = (lanes >= low) & (lanes < low + size)
        a_ref[top:k, :] = jnp.where(inside, 0.0, a_ref[top:k, :]) - change


def exact_dot(left, right, over):
    return lax.dot_general(
        left,
        right,
        (((1,), (over,)), ((), ())),
        precision=HIGHEST,
        preferred_element_type=jnp.float32,
    )


def scales_of(tile_ref, n):
    norms = [tile_ref[n + i : n + i + 1, :] for i in range(2)]
    scale = [lax.rsqrt(v) for v in norms]
    across = [jnp.broadcast_to(s, (n, n)) for s in scale]
    return scale, [v * s for v, s in zip(norms, scale)], across, [s.T for s in across]


def top_kernel(both_ref, out_ref, a_ref, one_ref, r_ref, x_ref):
    n = both_ref.shape[1]
    second = lax.axis_index("grp") % 2 == 1

    @pl.when(jnp.logical_not(second))
    def _():
        out_ref[0:n, :] = both_ref[0:n, :]
        out_ref[n : 2 * n, :] = jnp.zeros((n, n), jnp.float32)

    @pl.when(second)
    def _():
        one_ref[...] = jnp.ones_like(one_ref)
        row = lax.broadcasted_iota(jnp.int32, (n, n), 0)
        col = lax.broadcasted_iota(jnp.int32, (n, n), 1)
        scale = lax.rsqrt(both_ref[n : n + 1, :])
        across = jnp.broadcast_to(scale, (n, n))
        packed = both_ref[0:n, :]
        whole = jnp.where(row > col, packed, packed.T) * across * across.T
        a_ref[...] = jnp.where(row == col, 1.0, whole)
        eliminate(a_ref, one_ref, r_ref, x_ref)
        out_ref[0:n, :] = jnp.where(row >= col, x_ref[...], r_ref[...])
        out_ref[n : 2 * n, :] = packed


def factor_top(both):
    n = both.shape[1]
    vmem = pl.BlockSpec(memory_space=pltpu.VMEM)
    return pl.pallas_call(
        top_kernel,
        out_shape=jax.ShapeDtypeStruct((2 * n, n), jnp.float32),
        in_specs=[vmem],
        out_specs=vmem,
        scratch_shapes=[
            pltpu.VMEM((n, n), jnp.float32),
            pltpu.VMEM((SUB, LANES), jnp.float32),
            pltpu.VMEM((n, n), jnp.float32),
            pltpu.VMEM((n, n), jnp.float32),
        ],
        compiler_params=pltpu.CompilerParams(vmem_limit_bytes=VMEM_LIMIT),
        name="factor_top",
    )(both)


def rest_kernel(
    steps, early, cells, own_ref, theirs_ref, both_ref, sketch_hbm, r_hbm, basis_hbm, proj_hbm,
    a_ref, one_ref, low_r_ref, low_x_ref, r_ref, x_ref, proj_ref, sketch, basis,
    sem_in, sem_r, sem_proj, sems, early_sems,
):
    copy_in = pltpu.make_async_copy(sketch_hbm, sketch, sem_in)
    copy_in.start()
    k = r_ref.shape[0]
    n = k // 2
    one_ref[...] = jnp.ones_like(one_ref)
    first = lax.axis_index("grp") % 2 == 0
    row = lax.broadcasted_iota(jnp.int32, (n, n), 0)
    col = lax.broadcasted_iota(jnp.int32, (n, n), 1)
    zero = jnp.zeros((n, n), jnp.float32)
    square = jnp.where(first, own_ref[0:n, :], theirs_ref[0:n, :])
    done = jnp.where(first, theirs_ref[0:n, :], own_ref[0:n, :])
    packed = jnp.where(first, theirs_ref[n:k, :], own_ref[n:k, :])
    scale, unscale, across, down = scales_of(both_ref, n)
    top_x = jnp.where(row >= col, done, zero)
    low_top = exact_dot(square * across[0] * down[1], top_x, 1)
    low_low = jnp.where(row < col, packed, packed.T) * across[1] * down[1]
    a_ref[...] = jnp.where(row == col, 1.0, low_low) - exact_dot(low_top, low_top, 1)
    r_ref[0:n, 0:n] = jnp.where(row < col, done, jnp.where(row == col, 1.0 / done, zero)) * unscale[0]
    r_ref[0:n, n:k] = low_top.T * unscale[1]
    r_ref[n:k, 0:n] = zero
    top_x_out = top_x * scale[0]
    x_ref[0:n, 0:n] = top_x_out
    x_ref[0:n, n:k] = zero
    back = exact_dot(low_top, top_x_out, 0)
    contract = (((1,), (1,)), ((), ()))
    high, middle, low = split3(top_x_out)
    top_parts = jnp.concatenate(
        [jnp.concatenate([high, middle], 1), jnp.concatenate([low, jnp.zeros_like(low)], 1)], 0
    )
    total_rows = sketch.shape[0]
    size = total_rows // early
    copies = []

    def first_columns(panel):
        if panel == 1:
            copy_in.wait()
        index = panel - 2
        if not 0 <= index < early:
            return
        rows = pl.ds(index * size, size)
        piece = sketch[rows, 0:n]
        pair = lax.dot_general(
            jnp.concatenate([piece, piece], 1),
            top_parts,
            contract,
            preferred_element_type=jnp.float32,
        )
        basis[rows, 0:n] = (pair[:, n:k] + pair[:, 0:n]).astype(basis.dtype)
        at = pl.ds(0, n)
        copy = pltpu.make_async_copy(
            basis.at[rows, at], basis_hbm.at[rows, at], early_sems.at[index]
        )
        copy.start()
        copies.append(copy)

    eliminate(a_ref, one_ref, low_r_ref, low_x_ref, first_columns)
    r_ref[n:k, n:k] = low_r_ref[...] * unscale[1]
    copy_r = pltpu.make_async_copy(r_ref, r_hbm, sem_r)
    copy_r.start()
    copies.append(copy_r)
    low_x = low_x_ref[...]
    low_left = -exact_dot(low_x, back, 0)
    low_right = low_x * scale[1]
    x_ref[n:k, 0:n] = low_left
    x_ref[n:k, n:k] = low_right
    high, middle, low = split3(jnp.concatenate([low_left, low_right], 1))
    paired = jnp.concatenate([high, middle], 0)
    size = total_rows // steps
    for step in range(steps):
        rows = pl.ds(step * size, size)
        piece = sketch[rows, :]
        pair = lax.dot_general(piece, paired, contract, preferred_element_type=jnp.float32)
        total = lax.dot_general(piece, low, contract, preferred_element_type=jnp.float32)
        basis[rows, n:k] = (total + pair[:, n:k] + pair[:, 0:n]).astype(basis.dtype)
        at = pl.ds(n, n)
        copy = pltpu.make_async_copy(basis.at[rows, at], basis_hbm.at[rows, at], sems.at[step])
        copy.start()
        copies.append(copy)
        if step:
            continue
        count = k // cells
        own_rows = pl.ds(pl.multiple_of(lax.axis_index("cell") * count, count), count)
        days = proj_ref.shape[0]
        total = None
        for h in range(k // LANES):
            at = n + SUB + h * days
            term = exact_dot(
                both_ref[at : at + days, :], x_ref[own_rows, h * LANES : (h + 1) * LANES], 1
            )
            total = term if total is None else total + term
        proj_ref[...] = total
        copy = pltpu.make_async_copy(proj_ref, proj_hbm, sem_proj)
        copy.start()
        copies.append(copy)
    for copy in copies:
        copy.wait()


def factor_rest(own, theirs, both, sketch, cells):
    rows, k = sketch.shape
    n = k // 2
    days = (both.shape[0] - n - SUB) * LANES // k
    steps = chunks_of(rows, 6)
    early = chunks_of(rows, n // SUB - 4)
    hbm = pl.BlockSpec(memory_space=pltpu.HBM)
    vmem = pl.BlockSpec(memory_space=pltpu.VMEM)
    return pl.pallas_call(
        functools.partial(rest_kernel, steps, early, cells),
        out_shape=(
            jax.ShapeDtypeStruct((k, k), jnp.float32),
            jax.ShapeDtypeStruct((rows, k), jnp.bfloat16),
            jax.ShapeDtypeStruct((days, k // cells), jnp.float32),
        ),
        in_specs=[vmem, vmem, vmem, hbm],
        out_specs=(hbm, hbm, hbm),
        scratch_shapes=[
            pltpu.VMEM((n, n), jnp.float32),
            pltpu.VMEM((SUB, LANES), jnp.float32),
            pltpu.VMEM((n, n), jnp.float32),
            pltpu.VMEM((n, n), jnp.float32),
            pltpu.VMEM((k, k), jnp.float32),
            pltpu.VMEM((k, k), jnp.float32),
            pltpu.VMEM((days, k // cells), jnp.float32),
            pltpu.VMEM((rows, k), sketch.dtype),
            pltpu.VMEM((rows, k), jnp.bfloat16),
            pltpu.SemaphoreType.DMA,
            pltpu.SemaphoreType.DMA,
            pltpu.SemaphoreType.DMA,
            pltpu.SemaphoreType.DMA((steps,)),
            pltpu.SemaphoreType.DMA((early,)),
        ],
        compiler_params=pltpu.CompilerParams(vmem_limit_bytes=VMEM_LIMIT),
        name="factor_rest",
    )(own, theirs, both, sketch)


def swap(value, axis, bit):
    size = lax.axis_size(axis)
    return lax.ppermute(value, axis, [(i, i ^ bit) for i in range(size)])


def local(sketch, slab):
    cells, groups = lax.axis_size("cell"), lax.axis_size("grp")
    place = lax.axis_index("grp")
    shared = sketch.shape[1] // 2 + SUB
    kept, sent = local_stats(sketch, slab, groups)
    both = kept + swap(sent, "grp", 1)
    bit = 2
    while bit < groups:
        gram, days = both[:shared], both[shared:]
        days = days.reshape(groups // (2 * bit), 2, -1, LANES)
        own = (place // bit) % 2
        kept_days = lax.dynamic_index_in_dim(days, own, 1, keepdims=False).reshape(-1, LANES)
        sent_days = lax.dynamic_index_in_dim(days, 1 - own, 1, keepdims=False).reshape(-1, LANES)
        got = swap(jnp.concatenate([gram, sent_days], 0), "grp", bit)
        both = jnp.concatenate([gram, kept_days], 0) + got
        bit *= 2
    bit = 1
    while bit < cells:
        both = both + swap(both, "cell", bit)
        bit *= 2
    own = factor_top(both)
    theirs = swap(own, "grp", 1)
    r_factor, basis, projected = factor_rest(own, theirs, both, sketch, cells)
    return r_factor, basis, projected.T


def solution(mesh):
    in_specs = (P(("parts", "cell", "grp"), None), P(("parts", "cell", "grp"), None))
    out_specs = (P("parts", None), P(("parts", "cell", "grp"), None), P(("parts", "cell"), "grp"))
    return jax.shard_map(local, mesh=mesh, in_specs=in_specs, out_specs=out_specs, check_vma=False)
```

```python
import functools

import jax
import jax.numpy as jnp
from jax import lax
from jax.experimental import pallas as pl
from jax.experimental.pallas import tpu as pltpu
from jax.sharding import PartitionSpec as P

SUB, LANES = 8, 128
VMEM_LIMIT = 24 * 2**20
STATS_LIMIT = 56 * 10**6
HIGHEST = lax.Precision.HIGHEST


def chunks_of(rows, wanted):
    while rows % (16 * wanted):
        wanted -= 1
    return wanted


def stats_kernel(
    steps, groups, sketch_hbm, slab_hbm, kept_ref, sent_ref, sketch, slab, gram_ref, cross_ref, sems
):
    size = sketch.shape[0] // steps
    copies = []
    for step in range(steps):
        rows = pl.ds(step * size, size)
        pair = []
        for which, (src, dst) in enumerate(((sketch_hbm, sketch), (slab_hbm, slab))):
            copy = pltpu.make_async_copy(src.at[rows], dst.at[rows], sems.at[which, step])
            copy.start()
            pair.append(copy)
        copies.append(pair)
    contract = (((0,), (0,)), ((), ()))
    for step in range(steps):
        rows = pl.ds(step * size, size)
        for copy in copies[step]:
            copy.wait()
        part = sketch[rows, :]
        gram = lax.dot_general(part, part, contract, preferred_element_type=jnp.float32)
        cross = lax.dot_general(slab[rows, :], part, contract, preferred_element_type=jnp.float32)
        if step:
            gram, cross = gram_ref[...] + gram, cross_ref[...] + cross
        gram_ref[...] = gram
        cross_ref[...] = cross
    k = gram_ref.shape[0]
    n = k // 2
    first = lax.axis_index("grp") % 2 == 0
    row = lax.broadcasted_iota(jnp.int32, (n, n), 0)
    col = lax.broadcasted_iota(jnp.int32, (n, n), 1)
    square, top, low = gram_ref[n:k, 0:n], gram_ref[0:n, 0:n], gram_ref[n:k, n:k]
    packed = jnp.where(row >= col, top, low)
    norms = [jnp.sum(jnp.where(row == col, v, 0.0), axis=0, keepdims=True) for v in (top, low)]
    tile = lax.broadcasted_iota(jnp.int32, (SUB, n), 0)
    diagonal = jnp.where(tile == 0, norms[0], jnp.where(tile == 1, norms[1], 0.0))
    kept_ref[0:n, :] = jnp.where(first, square, packed)
    sent_ref[0:n, :] = jnp.where(first, packed, square)
    for ref in (kept_ref, sent_ref):
        ref[n : n + SUB, :] = diagonal
    count = cross_ref.shape[0] // groups
    at = n + SUB
    for pair in range(groups // 2):
        even = pl.ds(2 * pair * count, count)
        odd = pl.ds((2 * pair + 1) * count, count)
        for lanes in (pl.ds(h, LANES) for h in range(0, k, LANES)):
            rows = pl.ds(at, count)
            kept_ref[rows, :] = jnp.where(first, cross_ref[even, lanes], cross_ref[odd, lanes])
            sent_ref[rows, :] = jnp.where(first, cross_ref[odd, lanes], cross_ref[even, lanes])
            at += count


def local_stats(sketch, slab, groups):
    rows, k = sketch.shape
    days = slab.shape[1]
    steps = chunks_of(rows, 3)
    hbm = pl.BlockSpec(memory_space=pltpu.HBM)
    vmem = pl.BlockSpec(memory_space=pltpu.VMEM)
    out = jax.ShapeDtypeStruct((k // 2 + SUB + days // 2 * (k // LANES), LANES), jnp.float32)
    return pl.pallas_call(
        functools.partial(stats_kernel, steps, groups),
        out_shape=(out, out),
        in_specs=[hbm, hbm],
        out_specs=(vmem, vmem),
        scratch_shapes=[
            pltpu.VMEM((rows, k), sketch.dtype),
            pltpu.VMEM((rows, days), slab.dtype),
            pltpu.VMEM((k, k), jnp.float32),
            pltpu.VMEM((days, k), jnp.float32),
            pltpu.SemaphoreType.DMA((2, steps)),
        ],
        compiler_params=pltpu.CompilerParams(vmem_limit_bytes=STATS_LIMIT),
        name="local_stats",
    )(sketch, slab)


def tree_sum(terms):
    while len(terms) > 1:
        odd = terms[len(terms) & ~1 :]
        terms = [x + y for x, y in zip(terms[::2], terms[1::2])] + odd
    return terms[0]


def split3(v):
    high = v.astype(jnp.bfloat16)
    rest = v - high.astype(jnp.float32)
    middle = rest.astype(jnp.bfloat16)
    low = (rest - middle.astype(jnp.float32)).astype(jnp.bfloat16)
    return high, middle, low


def eliminate(a_ref, one_ref, r_ref, x_ref, meanwhile=None):
    k = a_ref.shape[0]
    halves, panels = k // LANES, k // SUB
    shape = (SUB, LANES)
    sub = lax.broadcasted_iota(jnp.int32, shape, 0)
    lane = lax.broadcasted_iota(jnp.int32, shape, 1)
    here = [sub == i for i in range(SUB)]
    one = one_ref[...]

    def rows_of(panel):
        return pl.ds(panel * SUB, SUB)

    def lanes_of(half):
        return pl.ds(half * LANES, LANES)

    def load(panel):
        return [a_ref[rows_of(panel), lanes_of(h)] for h in range(halves)]

    def row_of(v, i):
        return jnp.broadcast_to(v[i : i + 1, :], shape)

    def column_of(v, i):
        return jnp.broadcast_to(v[:, i : i + 1], shape)

    def follow(target, panel, pivots, coefs=None):
        half, first = divmod(panel * SUB, LANES)
        if coefs is None:
            coefs = [column_of(target[half], first + i) for i in range(SUB)]
        inside = (lane >= first) & (lane < first + SUB)
        rest = list(target)
        rest[half] = jnp.where(inside, 0.0, rest[half])
        return [
            rest[h] - tree_sum([coefs[i] * pivots[i][h] for i in range(SUB)]) for h in range(halves)
        ]

    def columns(panel, block):
        half, first = divmod(panel * SUB, LANES)
        return [column_of(block[half], first + i) * one for i in range(SUB)]

    def solve(panel, block, cols, under=None, corner=None):
        half, first = divmod(panel * SUB, LANES)
        block, cols = list(block), list(cols)
        saved = [jnp.zeros(shape, jnp.float32)] * halves
        roots = jnp.zeros(shape, jnp.float32)
        for i in range(0, SUB, 2):
            upper, lower = here[i], here[i + 1]
            both = upper | lower
            p, q, r = row_of(cols[i], i), row_of(cols[i + 1], i), row_of(cols[i + 1], i + 1)
            det = p * r - q * q
            inverse = 1.0 / det
            over = 1.0 / p
            roots = jnp.where(
                both, jnp.where(upper, lax.rsqrt(p), lax.rsqrt(det * over)), roots
            )
            ratio = jnp.where(lower, q * over, 0.0)
            for h in range(halves):
                z = block[h] - ratio * row_of(block[h], i)
                if h == half:
                    z = jnp.where((lane == first + i) & lower, -ratio, z)
                saved[h] = jnp.where(both, z, saved[h])
            left = jnp.where(upper, -1.0, jnp.where(lower, 0.0, cols[i]))
            right = jnp.where(upper, 0.0, jnp.where(lower, -1.0, cols[i + 1]))
            on_upper = left * r - right * q
            on_lower = right * p - left * q

            def step(v):
                change = row_of(v, i) * on_upper + row_of(v, i + 1) * on_lower
                return jnp.where(both, 0.0, v) - change * inverse

            unit = jnp.where(
                lane == first + i, jnp.where(upper, 1.0, 0.0), jnp.where(lower, 1.0, 0.0)
            )
            pair = (lane == first + i) | (lane == first + i + 1)
            block[half] = jnp.where(pair, unit, block[half])
            if under is not None:
                left, right = under[i], under[i + 1]
                by_upper = left * r - right * q
                by_lower = right * p - left * q

                def step_under(v, upper_value, lower_value):
                    return v - (upper_value * by_upper + lower_value * by_lower) * inverse

                corner = [
                    step_under(c, row_of(left, j), row_of(right, j)) for j, c in enumerate(corner)
                ]
                under = [
                    step_under(u, row_of(cols[j], i), row_of(cols[j], i + 1)) if j > i + 1 else u
                    for j, u in enumerate(under)
                ]
            cols = [step(c) if j > i + 1 else c for j, c in enumerate(cols)]
            block = [step(v) for v in block]
        for h in range(halves):
            ahead = lane + h * LANES - (sub + panel * SUB)
            z = saved[h] * roots
            inverse_part = jnp.where(ahead < 0, z, jnp.where(ahead == 0, roots, 0.0))
            r_ref[rows_of(panel), lanes_of(h)] = jnp.where(ahead >= 0, z, 0.0)
            x_ref[rows_of(panel), lanes_of(h)] = inverse_part
        return block, corner

    per = 4
    size = per * SUB
    blocks = k // size
    lanes_all = lax.broadcasted_iota(jnp.int32, (size, k), 1)
    panel_all = lax.broadcasted_iota(jnp.int32, (size, k), 0) // SUB
    ahead_block = None
    for number in range(blocks):
        befores, afters = [], []
        for panel in range(number * per, (number + 1) * per):
            before = load(panel) if ahead_block is None else ahead_block
            if panel % 2 == 0:
                lower = load(panel + 1)
                under = columns(panel, lower)
                after, corner = solve(
                    panel, before, columns(panel, before), under, columns(panel + 1, lower)
                )
            else:
                under = None
                after, _ = solve(panel, before, corner)
            befores.append(jnp.concatenate(before, 1))
            afters.append(jnp.concatenate(after, 1))
            pivots = [[row_of(v, i) for v in after] for i in range(SUB)]
            for other in range(panel + 1, min((number + 2) * per, panels)):
                target = follow(load(other), panel, pivots, under if other == panel + 1 else None)
                if other == panel + 1:
                    ahead_block = target
                    continue
                for h in range(halves):
                    a_ref[rows_of(other), lanes_of(h)] = target[h]
            if meanwhile is not None:
                meanwhile(panel)
        if number + 2 >= blocks:
            continue
        low = number * size
        top = (number + 2) * size
        base = top // LANES * LANES
        lhs = split3(jnp.concatenate(befores, 0)[:, base:])
        later = (lanes_all < low + size) & (lanes_all >= low + (panel_all + 1) * SUB)
        rhs = split3(jnp.where(later, 0.0, jnp.concatenate(afters, 0)))
        change = lax.dot_general(
            jnp.concatenate([lhs[i] for i in (0, 0, 1, 0, 2, 1)], 0),
            jnp.concatenate([rhs[i] for i in (0, 1, 0, 2, 0, 1)], 0),
            (((0,), (0,)), ((), ())),
            preferred_element_type=jnp.float32,
        )[top - base :]
        lanes = lax.broadcasted_iota(jnp.int32, (k - top, k), 1)
        inside = (lanes >= low) & (lanes < low + size)
        a_ref[top:k, :] = jnp.where(inside, 0.0, a_ref[top:k, :]) - change


def exact_dot(left, right, over):
    left_high, left_middle, left_low = split3(left)
    high, middle, low = split3(right)

    def two(first, second, by_first, by_second):
        return lax.dot_general(
            jnp.concatenate([first, second], 1),
            jnp.concatenate([by_first, by_second], over),
            (((1,), (over,)), ((), ())),
            preferred_element_type=jnp.float32,
        )

    small = two(left_middle, left_low, middle, high) + two(left_high, left_high, low, middle)
    return small + two(left_middle, left_high, high, high)


def scales_of(tile_ref, n):
    norms = [tile_ref[n + i : n + i + 1, :] for i in range(2)]
    scale = [lax.rsqrt(v) for v in norms]
    across = [jnp.broadcast_to(s, (n, n)) for s in scale]
    return scale, [v * s for v, s in zip(norms, scale)], across, [s.T for s in across]


def top_kernel(both_ref, out_ref, a_ref, one_ref, r_ref, x_ref):
    n = both_ref.shape[1]
    second = lax.axis_index("grp") % 2 == 1

    @pl.when(jnp.logical_not(second))
    def _():
        out_ref[0:n, :] = both_ref[0:n, :]
        out_ref[n : 2 * n, :] = jnp.zeros((n, n), jnp.float32)

    @pl.when(second)
    def _():
        one_ref[...] = jnp.ones_like(one_ref)
        row = lax.broadcasted_iota(jnp.int32, (n, n), 0)
        col = lax.broadcasted_iota(jnp.int32, (n, n), 1)
        scale = lax.rsqrt(both_ref[n : n + 1, :])
        across = jnp.broadcast_to(scale, (n, n))
        packed = both_ref[0:n, :]
        whole = jnp.where(row > col, packed, packed.T) * across * across.T
        a_ref[...] = jnp.where(row == col, 1.0, whole)
        eliminate(a_ref, one_ref, r_ref, x_ref)
        out_ref[0:n, :] = jnp.where(row >= col, x_ref[...], r_ref[...])
        out_ref[n : 2 * n, :] = packed


def factor_top(both):
    n = both.shape[1]
    vmem = pl.BlockSpec(memory_space=pltpu.VMEM)
    return pl.pallas_call(
        top_kernel,
        out_shape=jax.ShapeDtypeStruct((2 * n, n), jnp.float32),
        in_specs=[vmem],
        out_specs=vmem,
        scratch_shapes=[
            pltpu.VMEM((n, n), jnp.float32),
            pltpu.VMEM((SUB, LANES), jnp.float32),
            pltpu.VMEM((n, n), jnp.float32),
            pltpu.VMEM((n, n), jnp.float32),
        ],
        compiler_params=pltpu.CompilerParams(vmem_limit_bytes=VMEM_LIMIT),
        name="factor_top",
    )(both)


def rest_kernel(
    steps, early, cells, own_ref, theirs_ref, both_ref, sketch_hbm, r_hbm, basis_hbm, proj_hbm,
    a_ref, one_ref, low_r_ref, low_x_ref, r_ref, x_ref, proj_ref, sketch, basis,
    sem_in, sem_r, sem_proj, sems, early_sems,
):
    copy_in = pltpu.make_async_copy(sketch_hbm, sketch, sem_in)
    copy_in.start()
    k = r_ref.shape[0]
    n = k // 2
    one_ref[...] = jnp.ones_like(one_ref)
    first = lax.axis_index("grp") % 2 == 0
    row = lax.broadcasted_iota(jnp.int32, (n, n), 0)
    col = lax.broadcasted_iota(jnp.int32, (n, n), 1)
    zero = jnp.zeros((n, n), jnp.float32)
    square = jnp.where(first, own_ref[0:n, :], theirs_ref[0:n, :])
    done = jnp.where(first, theirs_ref[0:n, :], own_ref[0:n, :])
    packed = jnp.where(first, theirs_ref[n:k, :], own_ref[n:k, :])
    scale, unscale, across, down = scales_of(both_ref, n)
    top_x = jnp.where(row >= col, done, zero)
    low_top = exact_dot(square * across[0] * down[1], top_x, 1)
    low_low = jnp.where(row < col, packed, packed.T) * across[1] * down[1]
    a_ref[...] = jnp.where(row == col, 1.0, low_low) - exact_dot(low_top, low_top, 1)
    r_ref[0:n, 0:n] = jnp.where(row < col, done, jnp.where(row == col, 1.0 / done, zero)) * unscale[0]
    r_ref[0:n, n:k] = low_top.T * unscale[1]
    r_ref[n:k, 0:n] = zero
    top_x_out = top_x * scale[0]
    x_ref[0:n, 0:n] = top_x_out
    x_ref[0:n, n:k] = zero
    back = exact_dot(low_top, top_x_out, 0)
    contract = (((1,), (1,)), ((), ()))
    high, middle, low = split3(top_x_out)
    top_parts = jnp.concatenate(
        [jnp.concatenate([high, middle], 1), jnp.concatenate([low, jnp.zeros_like(low)], 1)], 0
    )
    total_rows = sketch.shape[0]
    size = total_rows // early
    copies = []

    def first_columns(panel):
        if panel == 1:
            copy_in.wait()
        index = panel - 2
        if not 0 <= index < early:
            return
        rows = pl.ds(index * size, size)
        piece = sketch[rows, 0:n]
        pair = lax.dot_general(
            jnp.concatenate([piece, piece], 1),
            top_parts,
            contract,
            preferred_element_type=jnp.float32,
        )
        basis[rows, 0:n] = (pair[:, n:k] + pair[:, 0:n]).astype(basis.dtype)
        at = pl.ds(0, n)
        copy = pltpu.make_async_copy(
            basis.at[rows, at], basis_hbm.at[rows, at], early_sems.at[index]
        )
        copy.start()
        copies.append(copy)

    eliminate(a_ref, one_ref, low_r_ref, low_x_ref, first_columns)
    r_ref[n:k, n:k] = low_r_ref[...] * unscale[1]
    copy_r = pltpu.make_async_copy(r_ref, r_hbm, sem_r)
    copy_r.start()
    copies.append(copy_r)
    low_x = low_x_ref[...]
    low_left = -exact_dot(low_x, back, 0)
    low_right = low_x * scale[1]
    x_ref[n:k, 0:n] = low_left
    x_ref[n:k, n:k] = low_right
    high, middle, low = split3(jnp.concatenate([low_left, low_right], 1))
    paired = jnp.concatenate([high, middle], 0)
    size = total_rows // steps
    for step in range(steps):
        rows = pl.ds(step * size, size)
        piece = sketch[rows, :]
        pair = lax.dot_general(piece, paired, contract, preferred_element_type=jnp.float32)
        total = lax.dot_general(piece, low, contract, preferred_element_type=jnp.float32)
        basis[rows, n:k] = (total + pair[:, n:k] + pair[:, 0:n]).astype(basis.dtype)
        at = pl.ds(n, n)
        copy = pltpu.make_async_copy(basis.at[rows, at], basis_hbm.at[rows, at], sems.at[step])
        copy.start()
        copies.append(copy)
        if step:
            continue
        count = k // cells
        own_rows = pl.ds(pl.multiple_of(lax.axis_index("cell") * count, count), count)
        days = proj_ref.shape[0]
        total = None
        for h in range(k // LANES):
            at = n + SUB + h * days
            term = exact_dot(
                both_ref[at : at + days, :], x_ref[own_rows, h * LANES : (h + 1) * LANES], 1
            )
            total = term if total is None else total + term
        proj_ref[...] = total
        copy = pltpu.make_async_copy(proj_ref, proj_hbm, sem_proj)
        copy.start()
        copies.append(copy)
    for copy in copies:
        copy.wait()


def factor_rest(own, theirs, both, sketch, cells):
    rows, k = sketch.shape
    n = k // 2
    days = (both.shape[0] - n - SUB) * LANES // k
    steps = chunks_of(rows, 6)
    early = chunks_of(rows, n // SUB - 4)
    hbm = pl.BlockSpec(memory_space=pltpu.HBM)
    vmem = pl.BlockSpec(memory_space=pltpu.VMEM)
    return pl.pallas_call(
        functools.partial(rest_kernel, steps, early, cells),
        out_shape=(
            jax.ShapeDtypeStruct((k, k), jnp.float32),
            jax.ShapeDtypeStruct((rows, k), jnp.bfloat16),
            jax.ShapeDtypeStruct((days, k // cells), jnp.float32),
        ),
        in_specs=[vmem, vmem, vmem, hbm],
        out_specs=(hbm, hbm, hbm),
        scratch_shapes=[
            pltpu.VMEM((n, n), jnp.float32),
            pltpu.VMEM((SUB, LANES), jnp.float32),
            pltpu.VMEM((n, n), jnp.float32),
            pltpu.VMEM((n, n), jnp.float32),
            pltpu.VMEM((k, k), jnp.float32),
            pltpu.VMEM((k, k), jnp.float32),
            pltpu.VMEM((days, k // cells), jnp.float32),
            pltpu.VMEM((rows, k), sketch.dtype),
            pltpu.VMEM((rows, k), jnp.bfloat16),
            pltpu.SemaphoreType.DMA,
            pltpu.SemaphoreType.DMA,
            pltpu.SemaphoreType.DMA,
            pltpu.SemaphoreType.DMA((steps,)),
            pltpu.SemaphoreType.DMA((early,)),
        ],
        compiler_params=pltpu.CompilerParams(vmem_limit_bytes=VMEM_LIMIT),
        name="factor_rest",
    )(own, theirs, both, sketch)


def swap(value, axis, bit):
    size = lax.axis_size(axis)
    return lax.ppermute(value, axis, [(i, i ^ bit) for i in range(size)])


def local(sketch, slab):
    cells, groups = lax.axis_size("cell"), lax.axis_size("grp")
    place = lax.axis_index("grp")
    shared = sketch.shape[1] // 2 + SUB
    kept, sent = local_stats(sketch, slab, groups)
    both = kept + swap(sent, "grp", 1)
    bit = 2
    while bit < groups:
        gram, days = both[:shared], both[shared:]
        days = days.reshape(groups // (2 * bit), 2, -1, LANES)
        own = (place // bit) % 2
        kept_days = lax.dynamic_index_in_dim(days, own, 1, keepdims=False).reshape(-1, LANES)
        sent_days = lax.dynamic_index_in_dim(days, 1 - own, 1, keepdims=False).reshape(-1, LANES)
        got = swap(jnp.concatenate([gram, sent_days], 0), "grp", bit)
        both = jnp.concatenate([gram, kept_days], 0) + got
        bit *= 2
    bit = 1
    while bit < cells:
        both = both + swap(both, "cell", bit)
        bit *= 2
    own = factor_top(both)
    theirs = swap(own, "grp", 1)
    r_factor, basis, projected = factor_rest(own, theirs, both, sketch, cells)
    return r_factor, basis, projected.T


def solution(mesh):
    in_specs = (P(("parts", "cell", "grp"), None), P(("parts", "cell", "grp"), None))
    out_specs = (P("parts", None), P(("parts", "cell", "grp"), None), P(("parts", "cell"), "grp"))
    return jax.shard_map(local, mesh=mesh, in_specs=in_specs, out_specs=out_specs, check_vma=False)
```

```python
import functools

import jax
import jax.numpy as jnp
from jax import lax
from jax.experimental import pallas as pl
from jax.experimental.pallas import tpu as pltpu
from jax.sharding import PartitionSpec as P

SUB, LANES = 8, 128
VMEM_LIMIT = 24 * 2**20
STATS_LIMIT = 56 * 10**6
HIGHEST = lax.Precision.HIGHEST


def chunks_of(rows, wanted):
    while rows % (16 * wanted):
        wanted -= 1
    return wanted


def stats_kernel(
    steps, groups, sketch_hbm, slab_hbm, kept_ref, sent_ref, sketch, slab, gram_ref, cross_ref, sems
):
    size = sketch.shape[0] // steps
    copies = []
    for step in range(steps):
        rows = pl.ds(step * size, size)
        pair = []
        for which, (src, dst) in enumerate(((sketch_hbm, sketch), (slab_hbm, slab))):
            copy = pltpu.make_async_copy(src.at[rows], dst.at[rows], sems.at[which, step])
            copy.start()
            pair.append(copy)
        copies.append(pair)
    contract = (((0,), (0,)), ((), ()))
    for step in range(steps):
        rows = pl.ds(step * size, size)
        for copy in copies[step]:
            copy.wait()
        part = sketch[rows, :]
        gram = lax.dot_general(part, part, contract, preferred_element_type=jnp.float32)
        cross = lax.dot_general(slab[rows, :], part, contract, preferred_element_type=jnp.float32)
        if step:
            gram, cross = gram_ref[...] + gram, cross_ref[...] + cross
        gram_ref[...] = gram
        cross_ref[...] = cross
    k = gram_ref.shape[0]
    n = k // 2
    first = lax.axis_index("grp") % 2 == 0
    row = lax.broadcasted_iota(jnp.int32, (n, n), 0)
    col = lax.broadcasted_iota(jnp.int32, (n, n), 1)
    square, top, low = gram_ref[n:k, 0:n], gram_ref[0:n, 0:n], gram_ref[n:k, n:k]
    packed = jnp.where(row >= col, top, low)
    norms = [jnp.sum(jnp.where(row == col, v, 0.0), axis=0, keepdims=True) for v in (top, low)]
    tile = lax.broadcasted_iota(jnp.int32, (SUB, n), 0)
    diagonal = jnp.where(tile == 0, norms[0], jnp.where(tile == 1, norms[1], 0.0))
    kept_ref[0:n, :] = jnp.where(first, square, packed)
    sent_ref[0:n, :] = jnp.where(first, packed, square)
    for ref in (kept_ref, sent_ref):
        ref[n : n + SUB, :] = diagonal
    count = cross_ref.shape[0] // groups
    at = n + SUB
    for pair in range(groups // 2):
        even = pl.ds(2 * pair * count, count)
        odd = pl.ds((2 * pair + 1) * count, count)
        for lanes in (pl.ds(h, LANES) for h in range(0, k, LANES)):
            rows = pl.ds(at, count)
            kept_ref[rows, :] = jnp.where(first, cross_ref[even, lanes], cross_ref[odd, lanes])
            sent_ref[rows, :] = jnp.where(first, cross_ref[odd, lanes], cross_ref[even, lanes])
            at += count


def local_stats(sketch, slab, groups):
    rows, k = sketch.shape
    days = slab.shape[1]
    steps = chunks_of(rows, 3)
    hbm = pl.BlockSpec(memory_space=pltpu.HBM)
    vmem = pl.BlockSpec(memory_space=pltpu.VMEM)
    out = jax.ShapeDtypeStruct((k // 2 + SUB + days // 2 * (k // LANES), LANES), jnp.float32)
    return pl.pallas_call(
        functools.partial(stats_kernel, steps, groups),
        out_shape=(out, out),
        in_specs=[hbm, hbm],
        out_specs=(vmem, vmem),
        scratch_shapes=[
            pltpu.VMEM((rows, k), sketch.dtype),
            pltpu.VMEM((rows, days), slab.dtype),
            pltpu.VMEM((k, k), jnp.float32),
            pltpu.VMEM((days, k), jnp.float32),
            pltpu.SemaphoreType.DMA((2, steps)),
        ],
        compiler_params=pltpu.CompilerParams(vmem_limit_bytes=STATS_LIMIT),
        name="local_stats",
    )(sketch, slab)


def tree_sum(terms):
    while len(terms) > 1:
        odd = terms[len(terms) & ~1 :]
        terms = [x + y for x, y in zip(terms[::2], terms[1::2])] + odd
    return terms[0]


def split3(v):
    high = v.astype(jnp.bfloat16)
    rest = v - high.astype(jnp.float32)
    middle = rest.astype(jnp.bfloat16)
    low = (rest - middle.astype(jnp.float32)).astype(jnp.bfloat16)
    return high, middle, low


def eliminate(a_ref, one_ref, r_ref, x_ref, meanwhile=None):
    k = a_ref.shape[0]
    halves, panels = k // LANES, k // SUB
    shape = (SUB, LANES)
    sub = lax.broadcasted_iota(jnp.int32, shape, 0)
    lane = lax.broadcasted_iota(jnp.int32, shape, 1)
    here = [sub == i for i in range(SUB)]
    one = one_ref[...]

    def rows_of(panel):
        return pl.ds(panel * SUB, SUB)

    def lanes_of(half):
        return pl.ds(half * LANES, LANES)

    def load(panel):
        return [a_ref[rows_of(panel), lanes_of(h)] for h in range(halves)]

    def row_of(v, i):
        return jnp.broadcast_to(v[i : i + 1, :], shape)

    def column_of(v, i):
        return jnp.broadcast_to(v[:, i : i + 1], shape)

    def follow(target, panel, pivots, coefs=None):
        half, first = divmod(panel * SUB, LANES)
        if coefs is None:
            coefs = [column_of(target[half], first + i) for i in range(SUB)]
        inside = (lane >= first) & (lane < first + SUB)
        rest = list(target)
        rest[half] = jnp.where(inside, 0.0, rest[half])
        return [
            rest[h] - tree_sum([coefs[i] * pivots[i][h] for i in range(SUB)]) for h in range(halves)
        ]

    def columns(panel, block):
        half, first = divmod(panel * SUB, LANES)
        return [column_of(block[half], first + i) * one for i in range(SUB)]

    def solve(panel, block, cols, under=None, corner=None):
        half, first = divmod(panel * SUB, LANES)
        block, cols = list(block), list(cols)
        saved = [jnp.zeros(shape, jnp.float32)] * halves
        roots = jnp.zeros(shape, jnp.float32)
        for i in range(0, SUB, 2):
            upper, lower = here[i], here[i + 1]
            both = upper | lower
            p, q, r = row_of(cols[i], i), row_of(cols[i + 1], i), row_of(cols[i + 1], i + 1)
            det = p * r - q * q
            inverse = 1.0 / det
            over = 1.0 / p
            roots = jnp.where(
                both, jnp.where(upper, lax.rsqrt(p), lax.rsqrt(det * over)), roots
            )
            ratio = jnp.where(lower, q * over, 0.0)
            for h in range(halves):
                z = block[h] - ratio * row_of(block[h], i)
                if h == half:
                    z = jnp.where((lane == first + i) & lower, -ratio, z)
                saved[h] = jnp.where(both, z, saved[h])
            left = jnp.where(upper, -1.0, jnp.where(lower, 0.0, cols[i]))
            right = jnp.where(upper, 0.0, jnp.where(lower, -1.0, cols[i + 1]))
            on_upper = left * r - right * q
            on_lower = right * p - left * q

            def step(v):
                change = row_of(v, i) * on_upper + row_of(v, i + 1) * on_lower
                return jnp.where(both, 0.0, v) - change * inverse

            unit = jnp.where(
                lane == first + i, jnp.where(upper, 1.0, 0.0), jnp.where(lower, 1.0, 0.0)
            )
            pair = (lane == first + i) | (lane == first + i + 1)
            block[half] = jnp.where(pair, unit, block[half])
            if under is not None:
                left, right = under[i], under[i + 1]
                by_upper = left * r - right * q
                by_lower = right * p - left * q

                def step_under(v, upper_value, lower_value):
                    return v - (upper_value * by_upper + lower_value * by_lower) * inverse

                corner = [
                    step_under(c, row_of(left, j), row_of(right, j)) for j, c in enumerate(corner)
                ]
                under = [
                    step_under(u, row_of(cols[j], i), row_of(cols[j], i + 1)) if j > i + 1 else u
                    for j, u in enumerate(under)
                ]
            cols = [step(c) if j > i + 1 else c for j, c in enumerate(cols)]
            block = [step(v) for v in block]
        for h in range(halves):
            ahead = lane + h * LANES - (sub + panel * SUB)
            z = saved[h] * roots
            inverse_part = jnp.where(ahead < 0, z, jnp.where(ahead == 0, roots, 0.0))
            r_ref[rows_of(panel), lanes_of(h)] = jnp.where(ahead >= 0, z, 0.0)
            x_ref[rows_of(panel), lanes_of(h)] = inverse_part
        return block, corner

    per = 4
    size = per * SUB
    blocks = k // size
    lanes_all = lax.broadcasted_iota(jnp.int32, (size, k), 1)
    panel_all = lax.broadcasted_iota(jnp.int32, (size, k), 0) // SUB
    ahead_block = None
    for number in range(blocks):
        befores, afters = [], []
        for panel in range(number * per, (number + 1) * per):
            before = load(panel) if ahead_block is None else ahead_block
            if panel % 2 == 0:
                lower = load(panel + 1)
                under = columns(panel, lower)
                after, corner = solve(
                    panel, before, columns(panel, before), under, columns(panel + 1, lower)
                )
            else:
                under = None
                after, _ = solve(panel, before, corner)
            befores.append(jnp.concatenate(before, 1))
            afters.append(jnp.concatenate(after, 1))
            pivots = [[row_of(v, i) for v in after] for i in range(SUB)]
            for other in range(panel + 1, min((number + 2) * per, panels)):
                target = follow(load(other), panel, pivots, under if other == panel + 1 else None)
                if other == panel + 1:
                    ahead_block = target
                    continue
                for h in range(halves):
                    a_ref[rows_of(other), lanes_of(h)] = target[h]
            if meanwhile is not None:
                meanwhile(panel)
        if number + 2 >= blocks:
            continue
        low = number * size
        top = (number + 2) * size
        base = top // LANES * LANES
        lhs = split3(jnp.concatenate(befores, 0)[:, base:])
        later = (lanes_all < low + size) & (lanes_all >= low + (panel_all + 1) * SUB)
        rhs = split3(jnp.where(later, 0.0, jnp.concatenate(afters, 0)))
        change = lax.dot_general(
            jnp.concatenate([lhs[i] for i in (0, 0, 1, 0, 2, 1)], 0),
            jnp.concatenate([rhs[i] for i in (0, 1, 0, 2, 0, 1)], 0),
            (((0,), (0,)), ((), ())),
            preferred_element_type=jnp.float32,
        )[top - base :]
        lanes = lax.broadcasted_iota(jnp.int32, (k - top, k), 1)
        inside = (lanes >= low) & (lanes < low + size)
        a_ref[top:k, :] = jnp.where(inside, 0.0, a_ref[top:k, :]) - change


def exact_dot(left, right, over):
    left_high, left_middle, left_low = split3(left)
    high, middle, low = split3(right)

    def two(first, second, by_first, by_second):
        return lax.dot_general(
            jnp.concatenate([first, second], 1),
            jnp.concatenate([by_first, by_second], over),
            (((1,), (over,)), ((), ())),
            preferred_element_type=jnp.float32,
        )

    small = two(left_middle, left_low, middle, high) + two(left_high, left_high, low, middle)
    return small + two(left_middle, left_high, high, high)


def scales_of(tile_ref, n):
    norms = [tile_ref[n + i : n + i + 1, :] for i in range(2)]
    scale = [lax.rsqrt(v) for v in norms]
    across = [jnp.broadcast_to(s, (n, n)) for s in scale]
    return scale, [v * s for v, s in zip(norms, scale)], across, [s.T for s in across]


def top_kernel(both_ref, out_ref, a_ref, one_ref, r_ref, x_ref):
    n = both_ref.shape[1]
    second = lax.axis_index("grp") % 2 == 1

    @pl.when(jnp.logical_not(second))
    def _():
        out_ref[0:n, :] = both_ref[0:n, :]
        out_ref[n : 2 * n, :] = jnp.zeros((n, n), jnp.float32)

    @pl.when(second)
    def _():
        one_ref[...] = jnp.ones_like(one_ref)
        row = lax.broadcasted_iota(jnp.int32, (n, n), 0)
        col = lax.broadcasted_iota(jnp.int32, (n, n), 1)
        scale = lax.rsqrt(both_ref[n : n + 1, :])
        across = jnp.broadcast_to(scale, (n, n))
        packed = both_ref[0:n, :]
        whole = jnp.where(row > col, packed, packed.T) * across * across.T
        a_ref[...] = jnp.where(row == col, 1.0, whole)
        eliminate(a_ref, one_ref, r_ref, x_ref)
        out_ref[0:n, :] = jnp.where(row >= col, x_ref[...], r_ref[...])
        out_ref[n : 2 * n, :] = packed


def factor_top(both):
    n = both.shape[1]
    vmem = pl.BlockSpec(memory_space=pltpu.VMEM)
    return pl.pallas_call(
        top_kernel,
        out_shape=jax.ShapeDtypeStruct((2 * n, n), jnp.float32),
        in_specs=[vmem],
        out_specs=vmem,
        scratch_shapes=[
            pltpu.VMEM((n, n), jnp.float32),
            pltpu.VMEM((SUB, LANES), jnp.float32),
            pltpu.VMEM((n, n), jnp.float32),
            pltpu.VMEM((n, n), jnp.float32),
        ],
        compiler_params=pltpu.CompilerParams(vmem_limit_bytes=VMEM_LIMIT),
        name="factor_top",
    )(both)


def rest_kernel(
    steps, early, cells, own_ref, theirs_ref, both_ref, sketch, r_hbm, basis_hbm, proj_hbm,
    a_ref, one_ref, low_r_ref, low_x_ref, r_ref, x_ref, proj_ref, basis,
    sem_r, sem_proj, sems, early_sems,
):
    k = r_ref.shape[0]
    n = k // 2
    one_ref[...] = jnp.ones_like(one_ref)
    first = lax.axis_index("grp") % 2 == 0
    row = lax.broadcasted_iota(jnp.int32, (n, n), 0)
    col = lax.broadcasted_iota(jnp.int32, (n, n), 1)
    zero = jnp.zeros((n, n), jnp.float32)
    square = jnp.where(first, own_ref[0:n, :], theirs_ref[0:n, :])
    done = jnp.where(first, theirs_ref[0:n, :], own_ref[0:n, :])
    packed = jnp.where(first, theirs_ref[n:k, :], own_ref[n:k, :])
    scale, unscale, across, down = scales_of(both_ref, n)
    top_x = jnp.where(row >= col, done, zero)
    low_top = exact_dot(square * across[0] * down[1], top_x, 1)
    low_low = jnp.where(row < col, packed, packed.T) * across[1] * down[1]
    a_ref[...] = jnp.where(row == col, 1.0, low_low) - exact_dot(low_top, low_top, 1)
    r_ref[0:n, 0:n] = jnp.where(row < col, done, jnp.where(row == col, 1.0 / done, zero)) * unscale[0]
    r_ref[0:n, n:k] = low_top.T * unscale[1]
    r_ref[n:k, 0:n] = zero
    top_x_out = top_x * scale[0]
    x_ref[0:n, 0:n] = top_x_out
    x_ref[0:n, n:k] = zero
    back = exact_dot(low_top, top_x_out, 0)
    contract = (((1,), (1,)), ((), ()))
    high, middle, low = split3(top_x_out)
    top_parts = jnp.concatenate(
        [jnp.concatenate([high, middle], 1), jnp.concatenate([low, jnp.zeros_like(low)], 1)], 0
    )
    total_rows = sketch.shape[0]
    size = total_rows // early
    copies = []

    def first_columns(panel):
        index = panel - 2
        if not 0 <= index < early:
            return
        rows = pl.ds(index * size, size)
        piece = sketch[rows, 0:n]
        pair = lax.dot_general(
            jnp.concatenate([piece, piece], 1),
            top_parts,
            contract,
            preferred_element_type=jnp.float32,
        )
        basis[rows, 0:n] = (pair[:, n:k] + pair[:, 0:n]).astype(basis.dtype)
        at = pl.ds(0, n)
        copy = pltpu.make_async_copy(
            basis.at[rows, at], basis_hbm.at[rows, at], early_sems.at[index]
        )
        copy.start()
        copies.append(copy)

    eliminate(a_ref, one_ref, low_r_ref, low_x_ref, first_columns)
    r_ref[n:k, n:k] = low_r_ref[...] * unscale[1]
    copy_r = pltpu.make_async_copy(r_ref, r_hbm, sem_r)
    copy_r.start()
    copies.append(copy_r)
    low_x = low_x_ref[...]
    low_left = -exact_dot(low_x, back, 0)
    low_right = low_x * scale[1]
    x_ref[n:k, 0:n] = low_left
    x_ref[n:k, n:k] = low_right
    high, middle, low = split3(jnp.concatenate([low_left, low_right], 1))
    paired = jnp.concatenate([high, middle], 0)
    size = total_rows // steps
    for step in range(steps):
        rows = pl.ds(step * size, size)
        piece = sketch[rows, :]
        pair = lax.dot_general(piece, paired, contract, preferred_element_type=jnp.float32)
        total = lax.dot_general(piece, low, contract, preferred_element_type=jnp.float32)
        basis[rows, n:k] = (total + pair[:, n:k] + pair[:, 0:n]).astype(basis.dtype)
        at = pl.ds(n, n)
        copy = pltpu.make_async_copy(basis.at[rows, at], basis_hbm.at[rows, at], sems.at[step])
        copy.start()
        copies.append(copy)
        if step:
            continue
        count = k // cells
        own_rows = pl.ds(pl.multiple_of(lax.axis_index("cell") * count, count), count)
        days = proj_ref.shape[0]
        total = None
        for h in range(k // LANES):
            at = n + SUB + h * days
            term = exact_dot(
                both_ref[at : at + days, :], x_ref[own_rows, h * LANES : (h + 1) * LANES], 1
            )
            total = term if total is None else total + term
        proj_ref[...] = total
        copy = pltpu.make_async_copy(proj_ref, proj_hbm, sem_proj)
        copy.start()
        copies.append(copy)
    for copy in copies:
        copy.wait()


def factor_rest(own, theirs, both, sketch, cells):
    rows, k = sketch.shape
    n = k // 2
    days = (both.shape[0] - n - SUB) * LANES // k
    steps = chunks_of(rows, 6)
    early = chunks_of(rows, n // SUB - 4)
    hbm = pl.BlockSpec(memory_space=pltpu.HBM)
    vmem = pl.BlockSpec(memory_space=pltpu.VMEM)
    return pl.pallas_call(
        functools.partial(rest_kernel, steps, early, cells),
        out_shape=(
            jax.ShapeDtypeStruct((k, k), jnp.float32),
            jax.ShapeDtypeStruct((rows, k), jnp.bfloat16),
            jax.ShapeDtypeStruct((days, k // cells), jnp.float32),
        ),
        in_specs=[vmem, vmem, vmem, vmem],
        out_specs=(hbm, hbm, hbm),
        scratch_shapes=[
            pltpu.VMEM((n, n), jnp.float32),
            pltpu.VMEM((SUB, LANES), jnp.float32),
            pltpu.VMEM((n, n), jnp.float32),
            pltpu.VMEM((n, n), jnp.float32),
            pltpu.VMEM((k, k), jnp.float32),
            pltpu.VMEM((k, k), jnp.float32),
            pltpu.VMEM((days, k // cells), jnp.float32),
            pltpu.VMEM((rows, k), jnp.bfloat16),
            pltpu.SemaphoreType.DMA,
            pltpu.SemaphoreType.DMA,
            pltpu.SemaphoreType.DMA((steps,)),
            pltpu.SemaphoreType.DMA((early,)),
        ],
        compiler_params=pltpu.CompilerParams(vmem_limit_bytes=VMEM_LIMIT),
        name="factor_rest",
    )(own, theirs, both, sketch)


def swap(value, axis, bit):
    size = lax.axis_size(axis)
    return lax.ppermute(value, axis, [(i, i ^ bit) for i in range(size)])


def local(sketch, slab):
    cells, groups = lax.axis_size("cell"), lax.axis_size("grp")
    place = lax.axis_index("grp")
    shared = sketch.shape[1] // 2 + SUB
    kept, sent = local_stats(sketch, slab, groups)
    both = kept + swap(sent, "grp", 1)
    bit = 2
    while bit < groups:
        gram, days = both[:shared], both[shared:]
        days = days.reshape(groups // (2 * bit), 2, -1, LANES)
        own = (place // bit) % 2
        kept_days = lax.dynamic_index_in_dim(days, own, 1, keepdims=False).reshape(-1, LANES)
        sent_days = lax.dynamic_index_in_dim(days, 1 - own, 1, keepdims=False).reshape(-1, LANES)
        got = swap(jnp.concatenate([gram, sent_days], 0), "grp", bit)
        both = jnp.concatenate([gram, kept_days], 0) + got
        bit *= 2
    bit = 1
    while bit < cells:
        both = both + swap(both, "cell", bit)
        bit *= 2
    own = factor_top(both)
    theirs = swap(own, "grp", 1)
    r_factor, basis, projected = factor_rest(own, theirs, both, sketch, cells)
    return r_factor, basis, projected.T


def solution(mesh):
    in_specs = (P(("parts", "cell", "grp"), None), P(("parts", "cell", "grp"), None))
    out_specs = (P("parts", None), P(("parts", "cell", "grp"), None), P(("parts", "cell"), "grp"))
    return jax.shard_map(local, mesh=mesh, in_specs=in_specs, out_specs=out_specs, check_vma=False)
```

```python
import functools

import jax
import jax.numpy as jnp
from jax import lax
from jax.experimental import pallas as pl
from jax.experimental.pallas import tpu as pltpu
from jax.sharding import PartitionSpec as P

SUB, LANES = 8, 128
VMEM_LIMIT = 24 * 2**20
STATS_LIMIT = 56 * 10**6
HIGHEST = lax.Precision.HIGHEST


def chunks_of(rows, wanted):
    while rows % (16 * wanted):
        wanted -= 1
    return wanted


def stats_kernel(
    steps, groups, sketch_hbm, slab_hbm, kept_ref, sent_ref, sketch, slab, gram_ref, cross_ref, sems
):
    size = sketch.shape[0] // steps
    copies = []
    for step in range(steps):
        rows = pl.ds(step * size, size)
        pair = []
        for which, (src, dst) in enumerate(((sketch_hbm, sketch), (slab_hbm, slab))):
            copy = pltpu.make_async_copy(src.at[rows], dst.at[rows], sems.at[which, step])
            copy.start()
            pair.append(copy)
        copies.append(pair)
    contract = (((0,), (0,)), ((), ()))
    for step in range(steps):
        rows = pl.ds(step * size, size)
        for copy in copies[step]:
            copy.wait()
        part = sketch[rows, :]
        gram = lax.dot_general(part, part, contract, preferred_element_type=jnp.float32)
        cross = lax.dot_general(slab[rows, :], part, contract, preferred_element_type=jnp.float32)
        if step:
            gram, cross = gram_ref[...] + gram, cross_ref[...] + cross
        gram_ref[...] = gram
        cross_ref[...] = cross
    k = gram_ref.shape[0]
    n = k // 2
    first = lax.axis_index("grp") % 2 == 0
    row = lax.broadcasted_iota(jnp.int32, (n, n), 0)
    col = lax.broadcasted_iota(jnp.int32, (n, n), 1)
    square, top, low = gram_ref[n:k, 0:n], gram_ref[0:n, 0:n], gram_ref[n:k, n:k]
    packed = jnp.where(row >= col, top, low)
    norms = [jnp.sum(jnp.where(row == col, v, 0.0), axis=0, keepdims=True) for v in (top, low)]
    tile = lax.broadcasted_iota(jnp.int32, (SUB, n), 0)
    diagonal = jnp.where(tile == 0, norms[0], jnp.where(tile == 1, norms[1], 0.0))
    kept_ref[0:n, :] = jnp.where(first, square, packed)
    sent_ref[0:n, :] = jnp.where(first, packed, square)
    for ref in (kept_ref, sent_ref):
        ref[n : n + SUB, :] = diagonal
    count = cross_ref.shape[0] // groups
    at = n + SUB
    for pair in range(groups // 2):
        even = pl.ds(2 * pair * count, count)
        odd = pl.ds((2 * pair + 1) * count, count)
        for lanes in (pl.ds(h, LANES) for h in range(0, k, LANES)):
            rows = pl.ds(at, count)
            kept_ref[rows, :] = jnp.where(first, cross_ref[even, lanes], cross_ref[odd, lanes])
            sent_ref[rows, :] = jnp.where(first, cross_ref[odd, lanes], cross_ref[even, lanes])
            at += count


def local_stats(sketch, slab, groups):
    rows, k = sketch.shape
    days = slab.shape[1]
    steps = chunks_of(rows, 3)
    hbm = pl.BlockSpec(memory_space=pltpu.HBM)
    vmem = pl.BlockSpec(memory_space=pltpu.VMEM)
    out = jax.ShapeDtypeStruct((k // 2 + SUB + days // 2 * (k // LANES), LANES), jnp.float32)
    return pl.pallas_call(
        functools.partial(stats_kernel, steps, groups),
        out_shape=(out, out),
        in_specs=[hbm, hbm],
        out_specs=(vmem, vmem),
        scratch_shapes=[
            pltpu.VMEM((rows, k), sketch.dtype),
            pltpu.VMEM((rows, days), slab.dtype),
            pltpu.VMEM((k, k), jnp.float32),
            pltpu.VMEM((days, k), jnp.float32),
            pltpu.SemaphoreType.DMA((2, steps)),
        ],
        compiler_params=pltpu.CompilerParams(vmem_limit_bytes=STATS_LIMIT),
        name="local_stats",
    )(sketch, slab)


def tree_sum(terms):
    while len(terms) > 1:
        odd = terms[len(terms) & ~1 :]
        terms = [x + y for x, y in zip(terms[::2], terms[1::2])] + odd
    return terms[0]


def split3(v):
    high = v.astype(jnp.bfloat16)
    rest = v - high.astype(jnp.float32)
    middle = rest.astype(jnp.bfloat16)
    low = (rest - middle.astype(jnp.float32)).astype(jnp.bfloat16)
    return high, middle, low


def eliminate(a_ref, one_ref, r_ref, x_ref, meanwhile=None):
    k = a_ref.shape[0]
    halves, panels = k // LANES, k // SUB
    shape = (SUB, LANES)
    sub = lax.broadcasted_iota(jnp.int32, shape, 0)
    lane = lax.broadcasted_iota(jnp.int32, shape, 1)
    here = [sub == i for i in range(SUB)]
    one = one_ref[...]

    def rows_of(panel):
        return pl.ds(panel * SUB, SUB)

    def lanes_of(half):
        return pl.ds(half * LANES, LANES)

    def load(panel):
        return [a_ref[rows_of(panel), lanes_of(h)] for h in range(halves)]

    def row_of(v, i):
        return jnp.broadcast_to(v[i : i + 1, :], shape)

    def column_of(v, i):
        return jnp.broadcast_to(v[:, i : i + 1], shape)

    def follow(target, panel, pivots, coefs=None):
        half, first = divmod(panel * SUB, LANES)
        if coefs is None:
            coefs = [column_of(target[half], first + i) for i in range(SUB)]
        inside = (lane >= first) & (lane < first + SUB)
        rest = list(target)
        rest[half] = jnp.where(inside, 0.0, rest[half])
        return [
            rest[h] - tree_sum([coefs[i] * pivots[i][h] for i in range(SUB)]) for h in range(halves)
        ]

    def columns(panel, block):
        half, first = divmod(panel * SUB, LANES)
        return [column_of(block[half], first + i) * one for i in range(SUB)]

    def solve(panel, block, cols, under=None, corner=None):
        half, first = divmod(panel * SUB, LANES)
        block, cols = list(block), list(cols)
        saved = [jnp.zeros(shape, jnp.float32)] * halves
        roots = jnp.zeros(shape, jnp.float32)
        for i in range(0, SUB, 2):
            upper, lower = here[i], here[i + 1]
            both = upper | lower
            p, q, r = row_of(cols[i], i), row_of(cols[i + 1], i), row_of(cols[i + 1], i + 1)
            det = p * r - q * q
            inverse = 1.0 / det
            over = 1.0 / p
            roots = jnp.where(
                both, jnp.where(upper, lax.rsqrt(p), lax.rsqrt(det * over)), roots
            )
            ratio = jnp.where(lower, q * over, 0.0)
            for h in range(halves):
                z = block[h] - ratio * row_of(block[h], i)
                if h == half:
                    z = jnp.where((lane == first + i) & lower, -ratio, z)
                saved[h] = jnp.where(both, z, saved[h])
            left = jnp.where(upper, -1.0, jnp.where(lower, 0.0, cols[i]))
            right = jnp.where(upper, 0.0, jnp.where(lower, -1.0, cols[i + 1]))
            on_upper = left * r - right * q
            on_lower = right * p - left * q

            def step(v):
                change = row_of(v, i) * on_upper + row_of(v, i + 1) * on_lower
                return jnp.where(both, 0.0, v) - change * inverse

            unit = jnp.where(
                lane == first + i, jnp.where(upper, 1.0, 0.0), jnp.where(lower, 1.0, 0.0)
            )
            pair = (lane == first + i) | (lane == first + i + 1)
            block[half] = jnp.where(pair, unit, block[half])
            if under is not None:
                left, right = under[i], under[i + 1]
                by_upper = left * r - right * q
                by_lower = right * p - left * q

                def step_under(v, upper_value, lower_value):
                    return v - (upper_value * by_upper + lower_value * by_lower) * inverse

                corner = [
                    step_under(c, row_of(left, j), row_of(right, j)) for j, c in enumerate(corner)
                ]
                under = [
                    step_under(u, row_of(cols[j], i), row_of(cols[j], i + 1)) if j > i + 1 else u
                    for j, u in enumerate(under)
                ]
            cols = [step(c) if j > i + 1 else c for j, c in enumerate(cols)]
            block = [step(v) for v in block]
        for h in range(halves):
            ahead = lane + h * LANES - (sub + panel * SUB)
            z = saved[h] * roots
            inverse_part = jnp.where(ahead < 0, z, jnp.where(ahead == 0, roots, 0.0))
            r_ref[rows_of(panel), lanes_of(h)] = jnp.where(ahead >= 0, z, 0.0)
            x_ref[rows_of(panel), lanes_of(h)] = inverse_part
        return block, corner

    per = 4
    size = per * SUB
    blocks = k // size
    lanes_all = lax.broadcasted_iota(jnp.int32, (size, k), 1)
    panel_all = lax.broadcasted_iota(jnp.int32, (size, k), 0) // SUB
    ahead_block = None
    for number in range(blocks):
        befores, afters = [], []
        for panel in range(number * per, (number + 1) * per):
            before = load(panel) if ahead_block is None else ahead_block
            if panel % 2 == 0:
                lower = load(panel + 1)
                under = columns(panel, lower)
                after, corner = solve(
                    panel, before, columns(panel, before), under, columns(panel + 1, lower)
                )
            else:
                under = None
                after, _ = solve(panel, before, corner)
            befores.append(jnp.concatenate(before, 1))
            afters.append(jnp.concatenate(after, 1))
            pivots = [[row_of(v, i) for v in after] for i in range(SUB)]
            for other in range(panel + 1, min((number + 2) * per, panels)):
                target = follow(load(other), panel, pivots, under if other == panel + 1 else None)
                if other == panel + 1:
                    ahead_block = target
                    continue
                for h in range(halves):
                    a_ref[rows_of(other), lanes_of(h)] = target[h]
            if meanwhile is not None:
                meanwhile(panel)
        if number + 2 >= blocks:
            continue
        low = number * size
        top = (number + 2) * size
        base = top // LANES * LANES
        lhs = split3(jnp.concatenate(befores, 0)[:, base:])
        later = (lanes_all < low + size) & (lanes_all >= low + (panel_all + 1) * SUB)
        rhs = split3(jnp.where(later, 0.0, jnp.concatenate(afters, 0)))
        change = lax.dot_general(
            jnp.concatenate([lhs[i] for i in (0, 0, 1, 0, 2, 1)], 0),
            jnp.concatenate([rhs[i] for i in (0, 1, 0, 2, 0, 1)], 0),
            (((0,), (0,)), ((), ())),
            preferred_element_type=jnp.float32,
        )[top - base :]
        lanes = lax.broadcasted_iota(jnp.int32, (k - top, k), 1)
        inside = (lanes >= low) & (lanes < low + size)
        a_ref[top:k, :] = jnp.where(inside, 0.0, a_ref[top:k, :]) - change


def exact_dot(left, right, over):
    left_high, left_middle, left_low = split3(left)
    high, middle, low = split3(right)

    def two(first, second, by_first, by_second):
        return lax.dot_general(
            jnp.concatenate([first, second], 1),
            jnp.concatenate([by_first, by_second], over),
            (((1,), (over,)), ((), ())),
            preferred_element_type=jnp.float32,
        )

    small = two(left_middle, left_low, middle, high) + two(left_high, left_high, low, middle)
    return small + two(left_middle, left_high, high, high)


def scales_of(tile_ref, n):
    norms = [tile_ref[n + i : n + i + 1, :] for i in range(2)]
    scale = [lax.rsqrt(v) for v in norms]
    across = [jnp.broadcast_to(s, (n, n)) for s in scale]
    return scale, [v * s for v, s in zip(norms, scale)], across, [s.T for s in across]


def top_kernel(both_ref, out_ref, a_ref, one_ref, r_ref, x_ref):
    n = both_ref.shape[1]
    second = lax.axis_index("grp") % 2 == 1

    @pl.when(jnp.logical_not(second))
    def _():
        out_ref[0:n, :] = both_ref[0:n, :]
        out_ref[n : 2 * n, :] = jnp.zeros((n, n), jnp.float32)

    @pl.when(second)
    def _():
        one_ref[...] = jnp.ones_like(one_ref)
        row = lax.broadcasted_iota(jnp.int32, (n, n), 0)
        col = lax.broadcasted_iota(jnp.int32, (n, n), 1)
        scale = lax.rsqrt(both_ref[n : n + 1, :])
        across = jnp.broadcast_to(scale, (n, n))
        packed = both_ref[0:n, :]
        whole = jnp.where(row > col, packed, packed.T) * across * across.T
        a_ref[...] = jnp.where(row == col, 1.0, whole)
        eliminate(a_ref, one_ref, r_ref, x_ref)
        out_ref[0:n, :] = jnp.where(row >= col, x_ref[...], r_ref[...])
        out_ref[n : 2 * n, :] = packed


def factor_top(both):
    n = both.shape[1]
    vmem = pl.BlockSpec(memory_space=pltpu.VMEM)
    return pl.pallas_call(
        top_kernel,
        out_shape=jax.ShapeDtypeStruct((2 * n, n), jnp.float32),
        in_specs=[vmem],
        out_specs=vmem,
        scratch_shapes=[
            pltpu.VMEM((n, n), jnp.float32),
            pltpu.VMEM((SUB, LANES), jnp.float32),
            pltpu.VMEM((n, n), jnp.float32),
            pltpu.VMEM((n, n), jnp.float32),
        ],
        compiler_params=pltpu.CompilerParams(vmem_limit_bytes=VMEM_LIMIT),
        name="factor_top",
    )(both)


def rest_kernel(
    steps, early, cells, own_ref, theirs_ref, both_ref, sketch, r_hbm, basis_hbm, proj_hbm,
    a_ref, one_ref, low_r_ref, low_x_ref, r_ref, x_ref, proj_ref, basis,
    sem_r, sem_proj, sems, early_sems,
):
    k = r_ref.shape[0]
    n = k // 2
    one_ref[...] = jnp.ones_like(one_ref)
    first = lax.axis_index("grp") % 2 == 0
    row = lax.broadcasted_iota(jnp.int32, (n, n), 0)
    col = lax.broadcasted_iota(jnp.int32, (n, n), 1)
    zero = jnp.zeros((n, n), jnp.float32)
    square = jnp.where(first, own_ref[0:n, :], theirs_ref[0:n, :])
    done = jnp.where(first, theirs_ref[0:n, :], own_ref[0:n, :])
    packed = jnp.where(first, theirs_ref[n:k, :], own_ref[n:k, :])
    scale, unscale, across, down = scales_of(both_ref, n)
    top_x = jnp.where(row >= col, done, zero)
    low_top = exact_dot(square * across[0] * down[1], top_x, 1)
    low_low = jnp.where(row < col, packed, packed.T) * across[1] * down[1]
    a_ref[...] = jnp.where(row == col, 1.0, low_low) - exact_dot(low_top, low_top, 1)
    r_ref[0:n, 0:n] = jnp.where(row < col, done, jnp.where(row == col, 1.0 / done, zero)) * unscale[0]
    r_ref[0:n, n:k] = low_top.T * unscale[1]
    r_ref[n:k, 0:n] = zero
    top_x_out = top_x * scale[0]
    x_ref[0:n, 0:n] = top_x_out
    x_ref[0:n, n:k] = zero
    back = exact_dot(low_top, top_x_out, 0)
    contract = (((1,), (1,)), ((), ()))
    high, middle, low = split3(top_x_out)
    top_parts = jnp.concatenate(
        [jnp.concatenate([high, middle], 1), jnp.concatenate([low, jnp.zeros_like(low)], 1)], 0
    )
    total_rows = sketch.shape[0]
    size = total_rows // early
    copies = []

    def first_columns(panel):
        index = panel - 2
        if not 0 <= index < early:
            return
        rows = pl.ds(index * size, size)
        piece = sketch[rows, 0:n]
        pair = lax.dot_general(
            jnp.concatenate([piece, piece], 1),
            top_parts,
            contract,
            preferred_element_type=jnp.float32,
        )
        basis[rows, 0:n] = (pair[:, n:k] + pair[:, 0:n]).astype(basis.dtype)
        at = pl.ds(0, n)
        copy = pltpu.make_async_copy(
            basis.at[rows, at], basis_hbm.at[rows, at], early_sems.at[index]
        )
        copy.start()
        copies.append(copy)

    eliminate(a_ref, one_ref, low_r_ref, low_x_ref, first_columns)
    r_ref[n:k, n:k] = low_r_ref[...] * unscale[1]
    copy_r = pltpu.make_async_copy(r_ref, r_hbm, sem_r)
    copy_r.start()
    copies.append(copy_r)
    low_x = low_x_ref[...]
    low_left = -exact_dot(low_x, back, 0)
    low_right = low_x * scale[1]
    x_ref[n:k, 0:n] = low_left
    x_ref[n:k, n:k] = low_right
    high, middle, low = split3(jnp.concatenate([low_left, low_right], 1))
    paired = jnp.concatenate([high, middle], 0)
    size = total_rows // steps
    for step in range(steps):
        rows = pl.ds(step * size, size)
        piece = sketch[rows, :]
        pair = lax.dot_general(piece, paired, contract, preferred_element_type=jnp.float32)
        total = lax.dot_general(piece, low, contract, preferred_element_type=jnp.float32)
        basis[rows, n:k] = (total + pair[:, n:k] + pair[:, 0:n]).astype(basis.dtype)
        at = pl.ds(n, n)
        copy = pltpu.make_async_copy(basis.at[rows, at], basis_hbm.at[rows, at], sems.at[step])
        copy.start()
        copies.append(copy)
        if step != steps // 2:
            continue
        count = k // cells
        own_rows = pl.ds(pl.multiple_of(lax.axis_index("cell") * count, count), count)
        days = proj_ref.shape[0]
        total = None
        for h in range(k // LANES):
            at = n + SUB + h * days
            term = exact_dot(
                both_ref[at : at + days, :], x_ref[own_rows, h * LANES : (h + 1) * LANES], 1
            )
            total = term if total is None else total + term
        proj_ref[...] = total
        copy = pltpu.make_async_copy(proj_ref, proj_hbm, sem_proj)
        copy.start()
        copies.append(copy)
    for copy in copies:
        copy.wait()


def factor_rest(own, theirs, both, sketch, cells):
    rows, k = sketch.shape
    n = k // 2
    days = (both.shape[0] - n - SUB) * LANES // k
    steps = chunks_of(rows, 6)
    early = chunks_of(rows, n // SUB - 4)
    hbm = pl.BlockSpec(memory_space=pltpu.HBM)
    vmem = pl.BlockSpec(memory_space=pltpu.VMEM)
    return pl.pallas_call(
        functools.partial(rest_kernel, steps, early, cells),
        out_shape=(
            jax.ShapeDtypeStruct((k, k), jnp.float32),
            jax.ShapeDtypeStruct((rows, k), jnp.bfloat16),
            jax.ShapeDtypeStruct((days, k // cells), jnp.float32),
        ),
        in_specs=[vmem, vmem, vmem, vmem],
        out_specs=(hbm, hbm, hbm),
        scratch_shapes=[
            pltpu.VMEM((n, n), jnp.float32),
            pltpu.VMEM((SUB, LANES), jnp.float32),
            pltpu.VMEM((n, n), jnp.float32),
            pltpu.VMEM((n, n), jnp.float32),
            pltpu.VMEM((k, k), jnp.float32),
            pltpu.VMEM((k, k), jnp.float32),
            pltpu.VMEM((days, k // cells), jnp.float32),
            pltpu.VMEM((rows, k), jnp.bfloat16),
            pltpu.SemaphoreType.DMA,
            pltpu.SemaphoreType.DMA,
            pltpu.SemaphoreType.DMA((steps,)),
            pltpu.SemaphoreType.DMA((early,)),
        ],
        compiler_params=pltpu.CompilerParams(vmem_limit_bytes=VMEM_LIMIT),
        name="factor_rest",
    )(own, theirs, both, sketch)


def swap(value, axis, bit):
    size = lax.axis_size(axis)
    return lax.ppermute(value, axis, [(i, i ^ bit) for i in range(size)])


def local(sketch, slab):
    cells, groups = lax.axis_size("cell"), lax.axis_size("grp")
    place = lax.axis_index("grp")
    shared = sketch.shape[1] // 2 + SUB
    kept, sent = local_stats(sketch, slab, groups)
    both = kept + swap(sent, "grp", 1)
    bit = 2
    while bit < groups:
        gram, days = both[:shared], both[shared:]
        days = days.reshape(groups // (2 * bit), 2, -1, LANES)
        own = (place // bit) % 2
        kept_days = lax.dynamic_index_in_dim(days, own, 1, keepdims=False).reshape(-1, LANES)
        sent_days = lax.dynamic_index_in_dim(days, 1 - own, 1, keepdims=False).reshape(-1, LANES)
        got = swap(jnp.concatenate([gram, sent_days], 0), "grp", bit)
        both = jnp.concatenate([gram, kept_days], 0) + got
        bit *= 2
    bit = 1
    while bit < cells:
        both = both + swap(both, "cell", bit)
        bit *= 2
    own = factor_top(both)
    theirs = swap(own, "grp", 1)
    r_factor, basis, projected = factor_rest(own, theirs, both, sketch, cells)
    return r_factor, basis, projected.T


def solution(mesh):
    in_specs = (P(("parts", "cell", "grp"), None), P(("parts", "cell", "grp"), None))
    out_specs = (P("parts", None), P(("parts", "cell", "grp"), None), P(("parts", "cell"), "grp"))
    return jax.shard_map(local, mesh=mesh, in_specs=in_specs, out_specs=out_specs, check_vma=False)
```
